128 devices in a mesh: ctx: 16 (over y, z_lo, core), tp: 8 (over x, z_hi).
Axes of the slice: x: 4, y: 4, z: 4 (z_hi: 2, z_lo: 2; z = z_hi * 2 + z_lo), core: 2. Of those that a mesh axis runs over, the one named last changes fastest.
Arguments:
- tokens: bfloat16 [2048, 16384], P('ctx', 'tp'), may hold values from -6 to 6
- kv_weight: bfloat16 [16384, 2048], P('tp'), may hold values from -0.0625 to 0.0625
- queries: bfloat16 [2048, 8192], P('ctx', 'tp'), may hold values from -8 to 8
- cache_keys: bfloat16 [32768, 1024], P('ctx', 'tp'), may hold values from -8 to 8
- cache_values: bfloat16 [32768, 1024], P('ctx', 'tp'), may hold values from -6 to 6
- cache_lengths: int32 [16], replicated, may hold values from 512 to 2048, as said below
- page_owner: int32 [64], replicated, may hold values from 0 to 15, as said below
- page_slot: int32 [64], replicated, may hold values from 0 to 7, as said below
Outputs:
- attended: bfloat16 [2048, 8192], P('ctx', 'tp')
- kv_pages: bfloat16 [4096, 2048], P('ctx', 'tp')
The draws below stay inside these ranges and needn't reach their ends.
Inputs may be any that keep to these rules, and one draw needn't show every extreme that they name: `page_owner`: each owner receives at most 8 pages, in distinct slots; some owner receives exactly 8 in every draw. `page_slot`: slots of pages with the same owner are distinct. `cache_lengths`: some owner is full in every draw.
All inputs are finite; a program needn't handle non-finite values.
Results may differ from the reference program's by a relative error of at most 0.035.
Values may be sent and summed in bfloat16 or wider, within the bound.
No kernel may reach another device: no remote copies, remote signals or barrier semaphores. Data moves between devices by JAX's collectives and lax.ppermute only.
A program may use at most 192 MiB of HBM per device.

```python
import math
import jax
import jax.numpy as jnp
from jax import lax

D = 16384
HD = 128
KVH = 8
QG = 8
PAGE = 32
CACHE_DEV = 2048
OWN_CAP = 8
TOKENS = 2048
PAGES = 64
OWNERS = 16
SLOTS_ALL = 128


def page_choice(key):
    key = jax.random.fold_in(key, 11)
    key_order, key_busy, key_mix = jax.random.split(key, 3)
    order = jax.random.permutation(key_order, SLOTS_ALL).astype(jnp.int32)
    busiest = jax.random.randint(key_busy, (), 0, SLOTS_ALL // OWN_CAP)
    slot_ids = jnp.arange(SLOTS_ALL, dtype=jnp.int32)
    priority = order - jnp.where(slot_ids // OWN_CAP == busiest, SLOTS_ALL, 0)
    chosen = jnp.argsort(priority, stable=True)[:PAGES]
    return chosen[jax.random.permutation(key_mix, PAGES)].astype(jnp.int32)


def draw_page_owner(key, part):
    chosen = page_choice(key)
    return (chosen // OWN_CAP).astype(jnp.int32)


def draw_page_slot(key, part):
    chosen = page_choice(key)
    return (chosen % OWN_CAP).astype(jnp.int32)


def draw_cache_lengths(key, part):
    key = jax.random.fold_in(key, 5)
    key_len, key_full = jax.random.split(key)
    lengths = jax.random.randint(key_len, (OWNERS,), CACHE_DEV // 4, CACHE_DEV + 1)
    fullest = jax.random.randint(key_full, (), 0, OWNERS)
    return jnp.where(jnp.arange(OWNERS) == fullest, CACHE_DEV, lengths).astype(jnp.int32)


def draw_queries(key, part):
    key = jax.random.fold_in(key, 3)
    values = jnp.clip(jax.random.normal(key, (TOKENS, KVH, QG, HD), jnp.float32), -6.0, 6.0)
    return values.reshape(TOKENS, KVH * QG * HD).astype(jnp.bfloat16)


def draw_cache_keys(key, part):
    key = jax.random.fold_in(key, 4)
    values = jnp.clip(jax.random.normal(key, (OWNERS, CACHE_DEV, KVH, HD), jnp.float32), -6.0, 6.0)
    return values.reshape(OWNERS * CACHE_DEV, KVH * HD).astype(jnp.bfloat16)


def with_spikes(drawn, stream_key, source, target, shards_of, factor):
    owner, partner = [(jnp.arange(drawn.shape[axis_at]) // (drawn.shape[axis_at] // shards_of)).reshape([-1 if axis == axis_at else 1 for axis in range(drawn.ndim)]) for axis_at in (source, target)]
    chosen = jax.random.permutation(stream_key, shards_of)[partner]
    strong = (owner == chosen) | (owner == (partner + shards_of // 2) % shards_of)
    return jnp.where(strong, factor * drawn, drawn)


def block_levels(stream_key, shape, cuts, low, top_value):
    loudness, own = 1.0, jax.random.fold_in(stream_key, 6)
    for dim, blocks in cuts:
        heights = jnp.exp(jax.random.uniform(jax.random.fold_in(own, dim), (blocks,), jnp.float32, low / len(cuts), top_value / len(cuts)))
        loudness = loudness * jnp.repeat(heights, shape[dim] // blocks).reshape([-1 if axis == dim else 1 for axis in range(len(shape))])
    return loudness


def centred(key, shape, deviation, reach, pieces=(), held_as=jnp.bfloat16):
    entries = deviation * jax.random.normal(key, shape, jnp.float32)
    if pieces:
        entries = entries * block_levels(key, shape, pieces, -0.22, 0.18)
    return jnp.clip(entries, -reach, reach).astype(held_as)


def heavy_noise(rng, dims, scale, bound, cuts, heavy, kind=jnp.bfloat16):
    drawn = scale * jax.random.normal(rng, dims, jnp.float32)
    if cuts:
        drawn = drawn * block_levels(rng, dims, cuts, -0.22, 0.18)
    return jnp.clip(with_spikes(drawn, jax.random.fold_in(rng, 3), *heavy), -bound, bound).astype(kind)


def setup_inputs(seed: int = 0) -> dict:
    seeds = jax.random.split(jax.random.key(seed), 9)
    return {
        "tokens": centred(seeds[0], (TOKENS, D), 1.0, 6.0, ((0, 16), (1, 8))),
        "kv_weight": heavy_noise(seeds[1], (D, KVH * 2 * HD), D ** -0.5, 0.0625, ((0, 8),), (0, 1, 8, 2.0)),
        "queries": draw_queries(jax.random.fold_in(seeds[8], 71), 0),
        "cache_keys": draw_cache_keys(jax.random.fold_in(seeds[8], 71), 0),
        "cache_values": centred(seeds[4], (OWNERS * CACHE_DEV, KVH * HD), 1.0, 6.0, ((0, 16), (1, 8))),
        "cache_lengths": draw_cache_lengths(jax.random.fold_in(seeds[8], 71), 0),
        "page_owner": draw_page_owner(jax.random.fold_in(seeds[8], 71), 0),
        "page_slot": draw_page_slot(jax.random.fold_in(seeds[8], 71), 0),
    }


def reference(tokens, kv_weight, queries, cache_keys, cache_values, cache_lengths, page_owner, page_slot):
    fresh = jnp.dot(tokens, kv_weight, preferred_element_type=jnp.float32).astype(jnp.bfloat16)
    owner_ids = jnp.arange(OWNERS, dtype=jnp.int32)
    slot_ids = jnp.arange(OWN_CAP, dtype=jnp.int32)
    matches = ((page_owner[None, None, :] == owner_ids[:, None, None])
               & (page_slot[None, None, :] == slot_ids[None, :, None])).astype(jnp.float32)
    paged = fresh.reshape(PAGES, PAGE * KVH * 2 * HD).astype(jnp.float32)
    placed = jnp.einsum("osp,pc->osc", matches, paged, precision=lax.Precision.HIGHEST)
    kv_pages = placed.reshape(OWNERS * OWN_CAP * PAGE, KVH * 2 * HD).astype(jnp.bfloat16)

    fresh_heads = fresh.reshape(TOKENS, KVH, 2, HD)
    old_keys = cache_keys.reshape(OWNERS * CACHE_DEV, KVH, HD)
    old_values = cache_values.reshape(OWNERS * CACHE_DEV, KVH, HD)
    all_keys = jnp.concatenate([old_keys, fresh_heads[:, :, 0]], 0).transpose(1, 0, 2)
    all_values = jnp.concatenate([old_values, fresh_heads[:, :, 1]], 0).transpose(1, 0, 2)
    position = jnp.arange(OWNERS * CACHE_DEV, dtype=jnp.int32)
    owner_of = position // CACHE_DEV
    local_pos = position % CACHE_DEV
    old_codes = jnp.where(local_pos < cache_lengths[owner_of], -1, -2).astype(jnp.int32)
    key_codes = jnp.concatenate([old_codes, jnp.arange(TOKENS, dtype=jnp.int32)], 0)
    query_heads = queries.reshape(TOKENS, KVH, QG, HD).transpose(1, 0, 2, 3)
    query_pos = jnp.arange(TOKENS, dtype=jnp.int32)
    block_size = math.gcd(TOKENS, 256)
    blocks = TOKENS // block_size

    def one_head(inputs):
        head_queries, head_keys, head_values = inputs
        keys_wide = head_keys.astype(jnp.float32)
        values_wide = head_values.astype(jnp.float32)

        def one_block(block_pair):
            rows_now, pos_now = block_pair
            scores = jnp.einsum("rgd,kd->rgk", rows_now.astype(jnp.float32), keys_wide) * (HD ** -0.5)
            visible = (key_codes[None, :] == -1) | ((key_codes[None, :] >= 0) & (key_codes[None, :] <= pos_now[:, None]))
            scores = jnp.where(visible[:, None, :], scores, -1e30)
            row_top = jnp.max(scores, axis=-1, keepdims=True)
            weights = jnp.where(visible[:, None, :], jnp.exp(scores - row_top), 0.0)
            totals = jnp.sum(weights, axis=-1)
            rounded = lax.optimization_barrier(weights.astype(jnp.bfloat16)).astype(jnp.float32)
            return jnp.einsum("rgk,kd->rgd", rounded, values_wide) / totals[..., None]

        results = lax.map(one_block, (head_queries.reshape(blocks, block_size, QG, HD),
                                      query_pos.reshape(blocks, block_size)))
        return results.reshape(TOKENS, QG, HD)

    heads_out = lax.map(one_head, (query_heads, all_keys, all_values))
    attended = heads_out.transpose(1, 0, 2, 3).reshape(TOKENS, KVH * QG * HD).astype(jnp.bfloat16)
    return attended, kv_pages
```

```python
import functools

import jax
import jax.numpy as jnp
from jax import lax
from jax.experimental import pallas as pl
from jax.experimental.pallas import tpu as pltpu
from jax.sharding import PartitionSpec as P

PAGE = 32
HD = 128
LOG2E = 1.4426950408889634
SCALE = LOG2E / HD**0.5
BIG = 2.0**100
F32 = jnp.float32
BF16 = jnp.bfloat16
VMEM_LIMIT = 56 * 2**20


def nt_dot(a, b):
    return lax.dot_general(a, b, (((1,), (1,)), ((), ())), preferred_element_type=F32)


def nn_dot(a, b):
    return lax.dot_general(a, b, (((1,), (0,)), ((), ())), preferred_element_type=F32)


def vmem_spec():
    return pl.BlockSpec(memory_space=pltpu.VMEM)


def smem_spec():
    return pl.BlockSpec(memory_space=pltpu.SMEM)


def project_kernel(tok_ref, w_ref, out_ref):
    out_ref[0] = nn_dot(tok_ref[...], w_ref[...]).astype(BF16)


def project(tokens, kv_weight):
    rows, depth = tokens.shape
    heads = kv_weight.shape[1] // (2 * HD)
    return pl.pallas_call(
        project_kernel,
        grid=(heads,),
        in_specs=[
            pl.BlockSpec((rows, depth), lambda h: (0, 0)),
            pl.BlockSpec((depth, 2 * HD), lambda h: (0, h)),
        ],
        out_specs=pl.BlockSpec((1, rows, 2 * HD), lambda h: (h, 0, 0)),
        out_shape=jax.ShapeDtypeStruct((heads, rows, 2 * HD), BF16),
        compiler_params=pltpu.CompilerParams(vmem_limit_bytes=VMEM_LIMIT),
        cost_estimate=pl.CostEstimate(
            flops=2 * rows * depth * heads * 2 * HD,
            bytes_accessed=2 * depth * heads * 2 * HD,
            transcendentals=0,
        ),
        name="project",
    )(tokens, kv_weight)


def attend_kernel(cfg, *refs):
    nq, nseg, seg, owner_xor, base, shifts, state_in, fresh, final = cfg
    refs = list(refs)
    take = lambda n: [refs.pop(0) for _ in range(n)]
    (len_ref,) = take(1)
    q_refs = take(nq)
    k_refs = take(nseg)
    v_refs = take(nseg)
    f_refs = take(4) if fresh else []
    st_in = take(3) if state_in else []
    outs = take(1) if final else take(3)
    qb, kb, vb, acc, ll, mm, sems = refs
    me = lax.axis_index("ctx")
    my_y = me // 4
    my_q = me % 4
    step = pl.program_id(0)
    rows = qb.shape[0]
    groups = rows // 128

    copies = []
    for s in range(nseg):
        copies.append(
            pltpu.make_async_copy(k_refs[s], kb.at[pl.ds(s * seg, seg)], sems.at[2 * s])
        )
        copies.append(
            pltpu.make_async_copy(v_refs[s], vb.at[pl.ds(s * seg, seg)], sems.at[2 * s + 1])
        )

    @pl.when(step == 0)
    def _():
        for c in copies:
            c.start()
        if fresh:
            for d in range(4):
                at = pl.ds(pl.multiple_of(nseg * seg + (my_q ^ d) * 128, 128), 128)
                kb[at, :] = f_refs[d][:, :HD]
                vb[at, :] = f_refs[d][:, HD:]

    for i in range(nq):

        @pl.when(step == i)
        def _():
            for g in range(groups):
                qb[g * 128 : (g + 1) * 128, :] = q_refs[i][:, g * 128 : (g + 1) * 128]

    @pl.when(step == 0)
    def _():
        for c in copies:
            c.wait()

    if state_in:
        mm[...] = st_in[2][0]
    else:
        top = jnp.max(nt_dot(qb[...], kb[:256, :]), axis=-1, keepdims=True) * SCALE
        mm[...] = jnp.broadcast_to(top.astype(BF16).astype(F32), mm.shape)

    query_y = shifts[0]
    for i in range(1, nq):
        query_y = jnp.where(step == i, shifts[i], query_y)
    query_y = lax.rem(my_y + 4 - query_y, 4)

    def masked(vals, size, limit, slope, fill):
        col = lax.broadcasted_iota(jnp.int32, (rows, size), 1)
        row = lax.rem(lax.broadcasted_iota(jnp.int32, (rows, size), 0), 128)
        return jnp.where(col <= limit + row * slope, vals, fill)

    def accumulate(at, size, limit=None, slope=None):
        at = pl.ds(pl.multiple_of(at, 128), size)
        s = nt_dot(qb[...], kb[at, :])
        tops = jnp.concatenate([mm[...]] * (size // 128), axis=1)
        p = jnp.exp2(s * SCALE - tops)
        if limit is not None:
            p = masked(p, size, limit, slope, 0.0)
        acc[...] += nn_dot(p.astype(BF16), vb[at, :])
        total = ll[...]
        for g in range(size // 128):
            total = total + p[:, g * 128 : (g + 1) * 128]
        ll[...] = total

    def segment(s):
        owner = me ^ owner_xor[0]
        for i in range(1, nseg):
            owner = jnp.where(s == i, me ^ owner_xor[i], owner)
        if fresh:
            owner = jnp.minimum(owner, 15)
        length = jnp.clip(len_ref[owner] - base, 0, seg)
        whole = length // 512 * 512
        rest = length - whole
        limit = rest - 1
        slope = 0
        if fresh:
            is_fresh = s == nseg
            diagonal = query_y == my_y
            whole = jnp.where(is_fresh, jnp.where(query_y > my_y, 512, 0), whole)
            rest = jnp.where(is_fresh, jnp.where(diagonal, 512, 0), rest)
            limit = jnp.where(is_fresh, my_q * 128, limit)
            slope = jnp.where(is_fresh, 1, 0)
        return s * seg, whole, rest, limit, slope

    nsegs = nseg + (1 if fresh else 0)

    def sweep():
        acc[...] = jnp.zeros_like(acc)
        ll[...] = jnp.zeros_like(ll)

        def one(s, carry):
            start, whole, rest, limit, slope = segment(s)
            wide = whole // 1024

            def wide_step(j, c):
                accumulate(start + j * 1024, 1024)
                return c

            lax.fori_loop(0, wide, wide_step, 0)

            @pl.when(whole > wide * 1024)
            def _():
                accumulate(start + wide * 1024, 512)

            @pl.when(rest > 256)
            def _():
                accumulate(start + whole, 512, limit, slope)

            @pl.when((rest > 0) & (rest <= 256))
            def _():
                accumulate(start + whole, 256, limit, slope)

            return carry

        lax.fori_loop(0, nsegs, one, 0)

    def raise_tops():
        def one(s, carry):
            start, whole, rest, limit, slope = segment(s)

            def part(j, c):
                at = pl.ds(pl.multiple_of(start + j * 128, 128), 128)
                s_now = nt_dot(qb[...], kb[at, :]) * SCALE
                edge = jnp.where(
                    j * 128 < whole, 128, limit - (j * 128 - whole)
                )
                tilt = jnp.where(j * 128 < whole, 0, slope)
                s_now = masked(s_now, 128, edge, tilt, -3.0e38)
                top = jnp.max(s_now, axis=-1, keepdims=True)
                mm[...] = jnp.maximum(mm[...], top.astype(BF16).astype(F32))
                return c

            return lax.fori_loop(0, (whole + rest + 127) // 128, part, carry)

        lax.fori_loop(0, nsegs, one, 0)

    def attempt(turn):
        @pl.when(turn == 1)
        def _():
            raise_tops()

        sweep()
        fits = jnp.max(ll[...]) < BIG
        return jnp.where((turn == 0) & jnp.logical_not(fits), 1, 2)

    lax.while_loop(lambda turn: turn < 2, attempt, 0)

    if state_in:
        decay = jnp.exp2(st_in[2][0] - mm[...])
        acc[...] += st_in[0][0] * decay
        ll[...] += st_in[1][0] * decay
    if not final:
        outs[0][0] = acc[...]
        outs[1][0] = ll[...]
        outs[2][0] = mm[...]
        return
    out = outs[0]
    lane = lax.broadcasted_iota(jnp.int32, (128, 128), 1)
    side = jnp.zeros((128, 128), F32)
    for g in range(groups):
        part = slice(g * 128, (g + 1) * 128)
        out[0, :, part] = acc[part, :].astype(BF16)
        total = jnp.sum(ll[part, :], axis=-1, keepdims=True)
        high = total.astype(BF16).astype(F32)
        side = jnp.where(lane == g, mm[part, :], side)
        side = jnp.where(lane == 8 + g, high, side)
        side = jnp.where(lane == 16 + g, total - high, side)
    out[0, :, groups * 128 :] = side.astype(BF16)


def attend(lengths, qs, ks, vs, owner_xor, base, shifts, state=None, fresh=None, final=False, share=0.7):
    nq, nseg, seg = len(qs), len(ks), ks[0].shape[0]
    width = qs[0].shape[1]
    rows = width
    cfg = (nq, nseg, seg, owner_xor, base, shifts, state is not None, fresh is not None, final)
    state_spec = pl.BlockSpec((1, rows, HD), lambda i: (i, 0, 0))
    any_spec = pl.BlockSpec(memory_space=pl.ANY)
    args = [lengths, *qs, *ks, *vs]
    in_specs = [smem_spec()] + [vmem_spec()] * nq + [any_spec] * (2 * nseg)
    if fresh is not None:
        args += list(fresh)
        in_specs += [vmem_spec()] * 4
    if state is not None:
        args += list(state)
        in_specs += [state_spec] * 3
    if final:
        out_specs = [pl.BlockSpec((1, 128, width + 128), lambda i: (i, 0, 0))]
        out_shape = [jax.ShapeDtypeStruct((nq, 128, width + 128), BF16)]
    else:
        out_specs = [state_spec] * 3
        out_shape = [jax.ShapeDtypeStruct((nq, rows, HD), F32)] * 3
    keys = nseg * seg + (512 if fresh is not None else 0)
    return pl.pallas_call(
        functools.partial(attend_kernel, cfg),
        grid=(nq,),
        in_specs=in_specs,
        out_specs=out_specs,
        out_shape=out_shape,
        scratch_shapes=[
            pltpu.VMEM((rows, HD), BF16),
            pltpu.VMEM((keys, HD), BF16),
            pltpu.VMEM((keys, HD), BF16),
            pltpu.VMEM((rows, HD), F32),
            pltpu.VMEM((rows, HD), F32),
            pltpu.VMEM((rows, HD), F32),
            pltpu.SemaphoreType.DMA((2 * nseg,)),
        ],
        compiler_params=pltpu.CompilerParams(vmem_limit_bytes=VMEM_LIMIT),
        cost_estimate=pl.CostEstimate(
            flops=int(share * 8 * nq * rows * keys * HD),
            bytes_accessed=4 * keys * HD,
            transcendentals=0,
        ),
        name="attend",
    )(*args)


def merge_kernel(*refs):
    parts, out = refs[:-1], refs[-1]
    groups = out.shape[1] // 128
    sides = [r[0, :, groups * 128 :].astype(F32) for r in parts]
    for g in range(groups):
        tops = [s[:, g : g + 1] for s in sides]
        sums = [s[:, 8 + g : 9 + g] + s[:, 16 + g : 17 + g] for s in sides]
        top = functools.reduce(jnp.maximum, tops)
        scales = [jnp.exp2(t - top) for t in tops]
        total = sum(a * b for a, b in zip(scales, sums))
        part = slice(g * 128, (g + 1) * 128)
        mixed = sum(a * r[0, :, part].astype(F32) for a, r in zip(scales, parts))
        out[:, part] = (mixed / total).astype(BF16)


def merge(parts):
    rows, width = parts[0].shape[1:]
    return pl.pallas_call(
        merge_kernel,
        in_specs=[vmem_spec()] * len(parts),
        out_specs=vmem_spec(),
        out_shape=jax.ShapeDtypeStruct((rows, width - 128), BF16),
        compiler_params=pltpu.CompilerParams(vmem_limit_bytes=VMEM_LIMIT),
        name="merge",
    )(*parts)


def pages_kernel(owner_ref, slot_ref, *refs):
    quads, out = refs[:-1], refs[-1]
    me = lax.axis_index("ctx")
    my_y = me // 4
    my_q = me % 4
    out[...] = jnp.zeros_like(out)
    for k in range(4):
        block_y = lax.rem(my_y + 4 - k, 4)

        def one(i, carry):
            page = block_y * 16 + i

            @pl.when(owner_ref[page] == me)
            def _():
                src = (my_q ^ (i // 4)) * 128 + (i % 4) * PAGE
                dst = slot_ref[page] * PAGE
                out[pl.ds(pl.multiple_of(dst, PAGE), PAGE), :] = quads[k][
                    pl.ds(pl.multiple_of(src, PAGE), PAGE), :
                ]

            return carry

        lax.fori_loop(0, 16, one, 0)


def pick_pages(page_owner, page_slot, quads):
    return pl.pallas_call(
        pages_kernel,
        in_specs=[smem_spec()] * 2 + [vmem_spec()] * len(quads),
        out_specs=vmem_spec(),
        out_shape=jax.ShapeDtypeStruct((8 * PAGE, 2 * HD), BF16),
        compiler_params=pltpu.CompilerParams(vmem_limit_bytes=VMEM_LIMIT),
        name="pages",
    )(page_owner, page_slot, *quads)


def flip(x, bits):
    return lax.ppermute(x, "ctx", [(i, i ^ bits) for i in range(16)])


def turn(x, k):
    return lax.ppermute(x, "ctx", [(i, (i + 4 * k) % 16) for i in range(16)])


def body(
    tokens, kv_weight, queries, cache_keys, cache_values, cache_lengths, page_owner, page_slot
):
    half = cache_keys.shape[0] // 2
    others = {k: turn(queries, k) for k in (1, 3, 2)}
    k_core, v_core = flip(cache_keys, 1), flip(cache_values, 1)
    far = []
    for c in range(2):
        part = slice(c * half, (c + 1) * half)
        kz, vz = flip(cache_keys[part], 2), flip(cache_values[part], 2)
        far.append(((kz, flip(kz, 1)), (vz, flip(vz, 1))))

    partial = project(tokens, kv_weight)
    gathered = lax.all_to_all(partial, "tp", 0, 0, tiled=True)
    fresh0 = jnp.sum(gathered.astype(F32), axis=0).astype(BF16)
    fresh = [fresh0] + [flip(fresh0, d) for d in (1, 2, 3)]
    quad = jnp.concatenate(fresh, axis=0)
    quads = [quad] + [turn(quad, k) for k in (1, 2, 3)]
    kv_pages = pick_pages(page_owner, page_slot, quads)

    near_k, near_v = (cache_keys, k_core), (cache_values, v_core)
    own = attend(cache_lengths, [queries], near_k, near_v, (0, 1), 0, (0,))
    order = (1, 3, 2)
    rest = attend(
        cache_lengths, [others[k] for k in order], near_k, near_v, (0, 1), 0, order
    )
    rest = attend(
        cache_lengths, [others[k] for k in order], far[0][0], far[0][1], (2, 3), 0, order,
        state=rest,
    )
    (sent,) = attend(
        cache_lengths, [others[k] for k in order], far[1][0], far[1][1], (2, 3), half, order,
        state=rest, fresh=fresh, final=True,
    )
    back = [turn(sent[i : i + 1], 4 - k) for i, k in enumerate(order)]
    own = attend(
        cache_lengths, [queries], far[0][0], far[0][1], (2, 3), 0, (0,), state=own
    )
    (mine,) = attend(
        cache_lengths, [queries], far[1][0], far[1][1], (2, 3), half, (0,),
        state=own, fresh=fresh, final=True,
    )
    attended = merge([mine, *back])
    return (attended, kv_pages)


def solution(mesh):
    placed = (
        P("ctx", "tp"),
        P("tp", None),
        P("ctx", "tp"),
        P("ctx", "tp"),
        P("ctx", "tp"),
        P(),
        P(),
        P(),
    )
    return jax.shard_map(
        body,
        mesh=mesh,
        in_specs=placed,
        out_specs=(P("ctx", "tp"), P("ctx", "tp")),
        check_vma=False,
    )
```

```python
import functools

import jax
import jax.numpy as jnp
from jax import lax
from jax.experimental import pallas as pl
from jax.experimental.pallas import tpu as pltpu
from jax.sharding import PartitionSpec as P

PAGE = 32
HD = 128
LOG2E = 1.4426950408889634
SCALE = LOG2E / HD**0.5
BIG = 2.0**100
F32 = jnp.float32
BF16 = jnp.bfloat16
VMEM_LIMIT = 56 * 2**20
SMALL = pl.CostEstimate(flops=1000, bytes_accessed=1000, transcendentals=0)


def nt_dot(a, b):
    return lax.dot_general(a, b, (((1,), (1,)), ((), ())), preferred_element_type=F32)


def nn_dot(a, b):
    return lax.dot_general(a, b, (((1,), (0,)), ((), ())), preferred_element_type=F32)


def vmem_spec():
    return pl.BlockSpec(memory_space=pltpu.VMEM)


def smem_spec():
    return pl.BlockSpec(memory_space=pltpu.SMEM)


def project_kernel(tok_ref, w_ref, out_ref):
    out_ref[0] = nn_dot(tok_ref[...], w_ref[...]).astype(BF16)


def project(tokens, kv_weight):
    rows, depth = tokens.shape
    heads = kv_weight.shape[1] // (2 * HD)
    return pl.pallas_call(
        project_kernel,
        grid=(heads,),
        in_specs=[
            pl.BlockSpec((rows, depth), lambda h: (0, 0)),
            pl.BlockSpec((depth, 2 * HD), lambda h: (0, h)),
        ],
        out_specs=pl.BlockSpec((1, rows, 2 * HD), lambda h: (h, 0, 0)),
        out_shape=jax.ShapeDtypeStruct((heads, rows, 2 * HD), BF16),
        compiler_params=pltpu.CompilerParams(vmem_limit_bytes=VMEM_LIMIT),
        cost_estimate=SMALL,
        name="project",
    )(tokens, kv_weight)


def attend_kernel(cfg, *refs):
    nq, nseg, seg, owner_xor, state_in, fresh = cfg
    refs = list(refs)
    take = lambda n: [refs.pop(0) for _ in range(n)]
    (len_ref,) = take(1)
    q_refs = take(nq)
    kv_refs = take(nseg)
    f_refs = take(1) if fresh else []
    st_refs = take(nq) if state_in else []
    out, qb, kb, acc, ll, mm, st, sems = refs
    me = lax.axis_index("ctx")
    step = pl.program_id(0)
    rows = qb.shape[0]
    groups = rows // 128
    nsegs = nseg + len(f_refs)

    copies = [
        pltpu.make_async_copy(r, kb.at[pl.ds(s * seg, seg)], sems.at[s])
        for s, r in enumerate(kv_refs + f_refs)
    ]

    @pl.when(step == 0)
    def _():
        for c in copies:
            c.start()

    for i in range(nq):

        @pl.when(step == i)
        def _():
            for g in range(groups):
                qb[g * 128 : (g + 1) * 128, :] = q_refs[i][:, g * 128 : (g + 1) * 128]
            if state_in:
                st[...] = st_refs[i][0]

    @pl.when(step == 0)
    def _():
        copies[0].wait()

    if state_in:
        side_in = st[:, groups * 128 :].astype(F32)
        for g in range(groups):
            mm[g * 128 : (g + 1) * 128, :] = jnp.broadcast_to(side_in[:, g : g + 1], (128, 128))
    else:
        top = jnp.max(nt_dot(qb[...], kb[:256, :HD]), axis=-1, keepdims=True) * SCALE
        mm[...] = jnp.broadcast_to(top.astype(BF16).astype(F32), mm.shape)

    def masked(vals, size, limit, slope, fill):
        col = lax.broadcasted_iota(jnp.int32, (rows, size), 1)
        row = lax.rem(lax.broadcasted_iota(jnp.int32, (rows, size), 0), 128)
        return jnp.where(col <= limit + row * slope, vals, fill)

    def accumulate(at, size, limit=None, slope=None):
        at = pl.ds(pl.multiple_of(at, 128), size)
        s = nt_dot(qb[...], kb[at, :HD])
        tops = jnp.concatenate([mm[...]] * (size // 128), axis=1)
        p = jnp.exp2(s * SCALE - tops)
        if limit is not None:
            p = masked(p, size, limit, slope, 0.0)
        acc[...] += nn_dot(p.astype(BF16), kb[at, HD:])
        total = ll[...]
        for g in range(size // 128):
            total = total + p[:, g * 128 : (g + 1) * 128]
        ll[...] = total

    def segment(s):
        owner = me ^ owner_xor[0]
        for i in range(1, nseg):
            owner = jnp.where(s == i, me ^ owner_xor[i], owner)
        length = jnp.clip(len_ref[owner], 0, seg)
        whole = length // 512 * 512
        rest = length - whole
        limit = rest - 1
        slope = 0
        if fresh:
            is_fresh = s == nseg
            before = me * 128
            whole = jnp.where(is_fresh, before // 512 * 512, whole)
            rest = jnp.where(is_fresh, before - whole + 128, rest)
            limit = jnp.where(is_fresh, before - whole, limit)
            slope = jnp.where(is_fresh, 1, 0)
        return s * seg, whole, rest, limit, slope

    def sweep(turn):
        acc[...] = jnp.zeros_like(acc)
        ll[...] = jnp.zeros_like(ll)

        def one(s, carry):
            start, whole, rest, limit, slope = segment(s)

            for i in range(1, nsegs):

                @pl.when((s == i) & (step == 0) & (turn == 0))
                def _():
                    copies[i].wait()

            wide = whole // 1024

            def wide_step(j, c):
                accumulate(start + j * 1024, 1024)
                return c

            lax.fori_loop(0, wide, wide_step, 0)

            @pl.when(whole > wide * 1024)
            def _():
                accumulate(start + wide * 1024, 512)

            @pl.when(rest > 256)
            def _():
                accumulate(start + whole, 512, limit, slope)

            @pl.when((rest > 0) & (rest <= 256))
            def _():
                accumulate(start + whole, 256, limit, slope)

            return carry

        lax.fori_loop(0, nsegs, one, 0)

    def raise_tops():
        def one(s, carry):
            start, whole, rest, limit, slope = segment(s)

            def part(j, c):
                at = pl.ds(pl.multiple_of(start + j * 128, 128), 128)
                s_now = nt_dot(qb[...], kb[at, :HD]) * SCALE
                edge = jnp.where(j * 128 < whole, 128, limit - (j * 128 - whole))
                tilt = jnp.where(j * 128 < whole, 0, slope)
                s_now = masked(s_now, 128, edge, tilt, -3.0e38)
                top = jnp.max(s_now, axis=-1, keepdims=True)
                mm[...] = jnp.maximum(mm[...], top.astype(BF16).astype(F32))
                return c

            return lax.fori_loop(0, (whole + rest + 127) // 128, part, carry)

        lax.fori_loop(0, nsegs, one, 0)

    def attempt(turn):
        @pl.when(turn == 1)
        def _():
            raise_tops()

        sweep(turn)
        fits = jnp.max(ll[...]) < BIG
        return jnp.where((turn == 0) & jnp.logical_not(fits), 1, 2)

    lax.while_loop(lambda turn: turn < 2, attempt, 0)

    lane = lax.broadcasted_iota(jnp.int32, (128, 128), 1)
    side = jnp.zeros((128, 128), F32)
    for g in range(groups):
        part = slice(g * 128, (g + 1) * 128)
        mixed = acc[part, :]
        total = jnp.sum(ll[part, :], axis=-1, keepdims=True)
        top = mm[part, :]
        if state_in:
            decay = jnp.exp2(side_in[:, g : g + 1] - top)
            mixed = mixed + st[:, part].astype(F32) * decay
            total = total + (side_in[:, 8 + g : 9 + g] + side_in[:, 16 + g : 17 + g]) * decay
        out[0, :, part] = mixed.astype(BF16)
        high = total.astype(BF16).astype(F32)
        side = jnp.where(lane == g, top, side)
        side = jnp.where(lane == 8 + g, high, side)
        side = jnp.where(lane == 16 + g, total - high, side)
    out[0, :, groups * 128 :] = side.astype(BF16)


def attend(lengths, qs, kvs, owner_xor, state=None, fresh=None, flops=1000):
    nq, nseg, seg = len(qs), len(kvs), kvs[0].shape[0]
    width = qs[0].shape[1]
    rows = width
    cfg = (nq, nseg, seg, owner_xor, state is not None, fresh is not None)
    packed = pl.BlockSpec((1, 128, width + 128), lambda i: (i, 0, 0))
    any_spec = pl.BlockSpec(memory_space=pl.ANY)
    args = [lengths, *qs, *kvs]
    in_specs = [smem_spec()] + [vmem_spec()] * nq + [any_spec] * nseg
    if fresh is not None:
        args.append(fresh)
        in_specs.append(any_spec)
    if state is not None:
        args += [array for array, _ in state]
        in_specs += [
            pl.BlockSpec((1, 128, width + 128), functools.partial(lambda at, i: (at, 0, 0), at))
            for _, at in state
        ]
    nsegs = nseg + (fresh is not None)
    return pl.pallas_call(
        functools.partial(attend_kernel, cfg),
        grid=(nq,),
        in_specs=in_specs,
        out_specs=packed,
        out_shape=jax.ShapeDtypeStruct((nq, 128, width + 128), BF16),
        scratch_shapes=[
            pltpu.VMEM((rows, HD), BF16),
            pltpu.VMEM((nsegs * seg, 2 * HD), BF16),
            pltpu.VMEM((rows, HD), F32),
            pltpu.VMEM((rows, HD), F32),
            pltpu.VMEM((rows, HD), F32),
            pltpu.VMEM((128, width + 128), BF16),
            pltpu.SemaphoreType.DMA((nsegs,)),
        ],
        compiler_params=pltpu.CompilerParams(vmem_limit_bytes=VMEM_LIMIT),
        cost_estimate=pl.CostEstimate(flops=flops, bytes_accessed=1000, transcendentals=0),
        name="attend",
    )(*args)


def merge_kernel(*refs):
    parts, out = refs[:-1], refs[-1]
    groups = out.shape[1] // 128
    sides = [r[0, :, groups * 128 :].astype(F32) for r in parts]
    top = functools.reduce(jnp.maximum, sides)
    scales = [jnp.exp2(s - top) for s in sides]
    total = jnp.zeros_like(top)
    for w, s in zip(scales, sides):
        total = total + w * (pltpu.roll(s, 120, 1) + pltpu.roll(s, 112, 1))
    scales = [w / total for w in scales]
    for g in range(groups):
        part = slice(g * 128, (g + 1) * 128)
        mixed = sum(w[:, g : g + 1] * r[0, :, part].astype(F32) for w, r in zip(scales, parts))
        out[:, part] = mixed.astype(BF16)


def merge(parts):
    rows, width = parts[0][1].shape[1:]
    return pl.pallas_call(
        merge_kernel,
        grid=(1,),
        in_specs=[
            pl.BlockSpec((1, rows, width), functools.partial(lambda at, i: (at, 0, 0), at))
            for at, _ in parts
        ],
        out_specs=pl.BlockSpec((rows, width - 128), lambda i: (0, 0)),
        out_shape=jax.ShapeDtypeStruct((rows, width - 128), BF16),
        compiler_params=pltpu.CompilerParams(vmem_limit_bytes=VMEM_LIMIT),
        cost_estimate=SMALL,
        name="merge",
    )(*[p for _, p in parts])


def pages_kernel(owner_ref, slot_ref, fresh_ref, out):
    me = lax.axis_index("ctx")
    out[...] = jnp.zeros_like(out)

    def one(page, carry):
        @pl.when(owner_ref[page] == me)
        def _():
            src = pl.ds(pl.multiple_of(page * PAGE, PAGE), PAGE)
            dst = pl.ds(pl.multiple_of(slot_ref[page] * PAGE, PAGE), PAGE)
            out[dst, :] = fresh_ref[src, :]

        return carry

    lax.fori_loop(0, owner_ref.shape[0], one, 0)


def pick_pages(page_owner, page_slot, fresh):
    return pl.pallas_call(
        pages_kernel,
        in_specs=[smem_spec()] * 2 + [vmem_spec()],
        out_specs=vmem_spec(),
        out_shape=jax.ShapeDtypeStruct((8 * PAGE, 2 * HD), BF16),
        compiler_params=pltpu.CompilerParams(vmem_limit_bytes=VMEM_LIMIT),
        cost_estimate=SMALL,
        name="pages",
    )(page_owner, page_slot, fresh)


def flip(x, bits):
    return lax.ppermute(x, "ctx", [(i, i ^ bits) for i in range(16)])


def turn(x, k):
    return lax.ppermute(x, "ctx", [(i, (i + 4 * k) % 16) for i in range(16)])


def body(
    tokens, kv_weight, queries, cache_keys, cache_values, cache_lengths, page_owner, page_slot
):
    order = (1, 3, 2)
    others = [turn(queries, k) for k in order]
    own_kv = jnp.concatenate([cache_keys, cache_values], axis=1)
    far_kv = flip(own_kv, 2)
    core_kv = flip(own_kv, 1)

    partial = project(tokens, kv_weight)
    gathered = lax.all_to_all(partial, "tp", 0, 0, tiled=True)

    near, far = (0, 1), (2, 3)
    lengths, _ = lax.optimization_barrier((cache_lengths, partial))
    near0 = attend(lengths, [queries], (own_kv, core_kv), near)
    lengths, gathered, _ = lax.optimization_barrier((lengths, gathered, near0))
    fresh = jnp.sum(gathered.astype(F32), axis=0).astype(BF16)
    spread = jnp.broadcast_to(fresh[None], (16, *fresh.shape))
    fresh = lax.all_to_all(spread, "ctx", 0, 0, tiled=True).reshape(16 * 128, 2 * HD)
    kv_pages = pick_pages(page_owner, page_slot, fresh)
    near1 = attend(lengths, others[:2], (own_kv, core_kv), near)
    lengths, far_kv, _ = lax.optimization_barrier((lengths, far_kv, near1))
    both_kv = flip(far_kv, 1)
    near2 = attend(lengths, others[2:], (own_kv, core_kv), near, flops=2 * 10**10)
    sent = attend(
        lengths, others, (far_kv, both_kv), far, state=[(near1, 0), (near1, 1), (near2, 0)]
    )
    back = [turn(sent[i : i + 1], 4 - k) for i, k in enumerate(order)]
    lengths, _ = lax.optimization_barrier((lengths, sent))
    mine = attend(
        lengths, [queries], (far_kv, both_kv), far, state=[(near0, 0)], fresh=fresh
    )
    attended = merge([(0, mine), *[(0, b) for b in back]])
    return (attended, kv_pages)


def solution(mesh):
    placed = (
        P("ctx", "tp"),
        P("tp", None),
        P("ctx", "tp"),
        P("ctx", "tp"),
        P("ctx", "tp"),
        P(),
        P(),
        P(),
    )
    return jax.shard_map(
        body,
        mesh=mesh,
        in_specs=placed,
        out_specs=(P("ctx", "tp"), P("ctx", "tp")),
        check_vma=False,
    )
```

```python
import functools

import jax
import jax.numpy as jnp
from jax import lax
from jax.experimental import pallas as pl
from jax.experimental.pallas import tpu as pltpu
from jax.sharding import PartitionSpec as P

PAGE = 32
HD = 128
LOG2E = 1.4426950408889634
SCALE = LOG2E / HD**0.5
BIG = 2.0**100
F32 = jnp.float32
BF16 = jnp.bfloat16
VMEM_LIMIT = 63 * 2**20 + 2**19 + 2**18 + 2**17
SMALL = pl.CostEstimate(flops=1000, bytes_accessed=1000, transcendentals=0)


def nt_dot(a, b):
    return lax.dot_general(a, b, (((1,), (1,)), ((), ())), preferred_element_type=F32)


def nn_dot(a, b):
    return lax.dot_general(a, b, (((1,), (0,)), ((), ())), preferred_element_type=F32)


def vmem_spec():
    return pl.BlockSpec(memory_space=pltpu.VMEM)


def smem_spec():
    return pl.BlockSpec(memory_space=pltpu.SMEM)


def project_kernel(tok_ref, w_ref, out_ref):
    result = nn_dot(tok_ref[...], w_ref[...]).astype(BF16)
    for h in range(out_ref.shape[0]):
        out_ref[h] = result[:, h * 2 * HD : (h + 1) * 2 * HD]


def project(tokens, kv_weight):
    rows, depth = tokens.shape
    heads = kv_weight.shape[1] // (2 * HD)
    at_once = 2
    return pl.pallas_call(
        project_kernel,
        grid=(heads // at_once,),
        in_specs=[
            pl.BlockSpec((rows, depth), lambda h: (0, 0)),
            pl.BlockSpec((depth, at_once * 2 * HD), lambda h: (0, h)),
        ],
        out_specs=pl.BlockSpec((at_once, rows, 2 * HD), lambda h: (h, 0, 0)),
        out_shape=jax.ShapeDtypeStruct((heads, rows, 2 * HD), BF16),
        compiler_params=pltpu.CompilerParams(vmem_limit_bytes=VMEM_LIMIT),
        cost_estimate=SMALL,
        name="project",
    )(tokens, kv_weight)


def attend_kernel(cfg, *refs):
    nq, nseg, seg, owner_xor, state_in, fresh = cfg
    refs = list(refs)
    take = lambda n: [refs.pop(0) for _ in range(n)]
    (len_ref,) = take(1)
    q_refs = take(nq)
    kv_refs = take(nseg)
    f_refs = take(1) if fresh else []
    page_refs = take(2) if fresh else []
    st_refs = take(nq) if state_in else []
    outs = take(nq)
    pages_out = take(1) if fresh else []
    qs, qb, kb, acc, ll, mm, st, sems, q_sems, st_sems = refs
    me = lax.axis_index("ctx")
    step = pl.program_id(0)
    rows = qb.shape[0]
    groups = rows // 128
    nsegs = nseg + len(f_refs)

    copies = [
        pltpu.make_async_copy(r, kb.at[pl.ds(s * seg, seg)], sems.at[s])
        for s, r in enumerate(kv_refs + f_refs)
    ]

    q_copies = [
        pltpu.make_async_copy(r, qs.at[i], q_sems.at[i]) for i, r in enumerate(q_refs)
    ]
    st_copies = [
        pltpu.make_async_copy(r, st.at[i], st_sems.at[i]) for i, r in enumerate(st_refs)
    ]

    @pl.when(step == 0)
    def _():
        q_copies[0].start()
        for c in copies[:1] + q_copies[1:] + st_copies + copies[1:]:
            c.start()

    for i in range(nq):

        @pl.when(step == i)
        def _():
            q_copies[i].wait()
            if state_in:
                st_copies[i].wait()

    for g in range(groups):
        qb[g * 128 : (g + 1) * 128, :] = qs[step, :, g * 128 : (g + 1) * 128]

    @pl.when(step == 0)
    def _():
        copies[0].wait()

    if state_in:
        side_in = st[step, :, groups * 128 :].astype(F32)
        for g in range(groups):
            mm[g * 128 : (g + 1) * 128, :] = jnp.broadcast_to(side_in[:, g : g + 1], (128, 128))
    else:
        top = jnp.max(nt_dot(qb[...], kb[:256, :HD]), axis=-1, keepdims=True) * SCALE
        mm[...] = jnp.broadcast_to(top.astype(BF16).astype(F32), mm.shape)

    def masked(vals, size, limit, slope, fill):
        col = lax.broadcasted_iota(jnp.int32, (rows, size), 1)
        row = lax.rem(lax.broadcasted_iota(jnp.int32, (rows, size), 0), 128)
        return jnp.where(col <= limit + row * slope, vals, fill)

    def accumulate(at, size, limit=None, slope=None):
        at = pl.ds(pl.multiple_of(at, 128), size)
        s = nt_dot(qb[...], kb[at, :HD])
        tops = jnp.concatenate([mm[...]] * (size // 128), axis=1)
        p = jnp.exp2(s * SCALE - tops)
        if limit is not None:
            p = masked(p, size, limit, slope, 0.0)
        acc[...] += nn_dot(p.astype(BF16), kb[at, HD:])
        total = ll[...]
        for g in range(size // 128):
            total = total + p[:, g * 128 : (g + 1) * 128]
        ll[...] = total

    def segment(s):
        owner = me ^ owner_xor[0]
        for i in range(1, nseg):
            owner = jnp.where(s == i, me ^ owner_xor[i], owner)
        length = jnp.clip(len_ref[owner], 0, seg)
        whole = length // 512 * 512
        rest = length - whole
        limit = rest - 1
        slope = 0
        if fresh:
            is_fresh = s == nseg
            before = me * 128
            whole = jnp.where(is_fresh, before // 512 * 512, whole)
            rest = jnp.where(is_fresh, before - whole + 128, rest)
            limit = jnp.where(is_fresh, before - whole, limit)
            slope = jnp.where(is_fresh, 1, 0)
        return s * seg, whole, rest, limit, slope

    def sweep(turn):
        acc[...] = jnp.zeros_like(acc)
        ll[...] = jnp.zeros_like(ll)

        def one(s, carry):
            start, whole, rest, limit, slope = segment(s)

            for i in range(1, nsegs):

                @pl.when((s == i) & (step == 0) & (turn == 0))
                def _():
                    copies[i].wait()

            wide = whole // 1024

            def wide_step(j, c):
                accumulate(start + j * 1024, 1024)
                return c

            lax.fori_loop(0, wide, wide_step, 0)

            @pl.when(whole > wide * 1024)
            def _():
                accumulate(start + wide * 1024, 512)

            @pl.when(rest > 256)
            def _():
                accumulate(start + whole, 512, limit, slope)

            @pl.when((rest > 0) & (rest <= 256))
            def _():
                accumulate(start + whole, 256, limit, slope)

            return carry

        lax.fori_loop(0, nsegs, one, 0)

    def raise_tops():
        def one(s, carry):
            start, whole, rest, limit, slope = segment(s)

            def part(j, c):
                at = pl.ds(pl.multiple_of(start + j * 128, 128), 128)
                s_now = nt_dot(qb[...], kb[at, :HD]) * SCALE
                edge = jnp.where(j * 128 < whole, 128, limit - (j * 128 - whole))
                tilt = jnp.where(j * 128 < whole, 0, slope)
                s_now = masked(s_now, 128, edge, tilt, -3.0e38)
                top = jnp.max(s_now, axis=-1, keepdims=True)
                mm[...] = jnp.maximum(mm[...], top.astype(BF16).astype(F32))
                return c

            return lax.fori_loop(0, (whole + rest + 127) // 128, part, carry)

        lax.fori_loop(0, nsegs, one, 0)

    def attempt(turn):
        @pl.when(turn == 1)
        def _():
            raise_tops()

        sweep(turn)
        fits = jnp.max(ll[...]) < BIG
        return jnp.where((turn == 0) & jnp.logical_not(fits), 1, 2)

    lax.while_loop(lambda turn: turn < 2, attempt, 0)

    lane = lax.broadcasted_iota(jnp.int32, (128, 128), 1)

    def finish(out):
        side = jnp.zeros((128, 128), F32)
        for g in range(groups):
            part = slice(g * 128, (g + 1) * 128)
            mixed = acc[part, :]
            total = jnp.sum(ll[part, :], axis=-1, keepdims=True)
            top = mm[part, :]
            if state_in:
                decay = jnp.exp2(side_in[:, g : g + 1] - top)
                mixed = mixed + st[step, :, part].astype(F32) * decay
                total = total + (side_in[:, 8 + g : 9 + g] + side_in[:, 16 + g : 17 + g]) * decay
            out[:, part] = mixed.astype(BF16)
            high = total.astype(BF16).astype(F32)
            side = jnp.where(lane == g, top, side)
            side = jnp.where(lane == 8 + g, high, side)
            side = jnp.where(lane == 16 + g, total - high, side)
        out[:, groups * 128 :] = side.astype(BF16)

    for i in range(nq):

        @pl.when(step == i)
        def _():
            finish(outs[i])

    if fresh:
        owner_ref, slot_ref = page_refs
        (pages,) = pages_out
        pages[...] = jnp.zeros_like(pages)

        def one_page(page, carry):
            @pl.when(owner_ref[page] == me)
            def _():
                src = pl.ds(pl.multiple_of(nseg * seg + page * PAGE, PAGE), PAGE)
                dst = pl.ds(pl.multiple_of(slot_ref[page] * PAGE, PAGE), PAGE)
                pages[dst, :] = kb[src, :]

            return carry

        lax.fori_loop(0, owner_ref.shape[0], one_page, 0)


def attend(lengths, qs, kvs, owner_xor, state=None, fresh=None, pages=None, flops=1000):
    nq, nseg, seg = len(qs), len(kvs), kvs[0].shape[0]
    width = qs[0].shape[1]
    rows = width
    cfg = (nq, nseg, seg, owner_xor, state is not None, fresh is not None)
    any_spec = pl.BlockSpec(memory_space=pl.ANY)
    args = [lengths, *qs, *kvs]
    in_specs = [smem_spec()] + [any_spec] * (nq + nseg)
    out_specs = [pl.BlockSpec((128, width + 128), lambda i: (0, 0))] * nq
    out_shape = [jax.ShapeDtypeStruct((128, width + 128), BF16)] * nq
    if fresh is not None:
        args += [fresh, *pages]
        in_specs += [any_spec, smem_spec(), smem_spec()]
        out_specs.append(pl.BlockSpec((8 * PAGE, 2 * HD), lambda i: (0, 0)))
        out_shape.append(jax.ShapeDtypeStruct((8 * PAGE, 2 * HD), BF16))
    if state is not None:
        args += state
        in_specs += [any_spec] * nq
    nsegs = nseg + (fresh is not None)
    return pl.pallas_call(
        functools.partial(attend_kernel, cfg),
        grid=(nq,),
        in_specs=in_specs,
        out_specs=out_specs,
        out_shape=out_shape,
        scratch_shapes=[
            pltpu.VMEM((nq, 128, width), BF16),
            pltpu.VMEM((rows, HD), BF16),
            pltpu.VMEM((nsegs * seg, 2 * HD), BF16),
            pltpu.VMEM((rows, HD), F32),
            pltpu.VMEM((rows, HD), F32),
            pltpu.VMEM((rows, HD), F32),
            pltpu.VMEM((nq, 128, width + 128), BF16),
            pltpu.SemaphoreType.DMA((nsegs,)),
            pltpu.SemaphoreType.DMA((nq,)),
            pltpu.SemaphoreType.DMA((nq,)),
        ],
        compiler_params=pltpu.CompilerParams(vmem_limit_bytes=VMEM_LIMIT),
        cost_estimate=pl.CostEstimate(flops=flops, bytes_accessed=1000, transcendentals=0),
        name="attend",
    )(*args)


def merge_kernel(*refs):
    parts, out = refs[:-1], refs[-1]
    groups = out.shape[1] // 128
    sides = [r[:, groups * 128 :].astype(F32) for r in parts]
    top = functools.reduce(jnp.maximum, sides)
    scales = [jnp.exp2(s - top) for s in sides]
    total = jnp.zeros_like(top)
    for w, s in zip(scales, sides):
        total = total + w * (pltpu.roll(s, 120, 1) + pltpu.roll(s, 112, 1))
    scales = [w / total for w in scales]
    for g in range(groups):
        part = slice(g * 128, (g + 1) * 128)
        mixed = sum(w[:, g : g + 1] * r[:, part].astype(F32) for w, r in zip(scales, parts))
        out[:, part] = mixed.astype(BF16)


def merge(parts):
    rows, width = parts[0].shape
    return pl.pallas_call(
        merge_kernel,
        grid=(2,),
        in_specs=[pl.BlockSpec((rows // 2, width), lambda i: (i, 0))] * len(parts),
        out_specs=pl.BlockSpec((rows // 2, width - 128), lambda i: (i, 0)),
        out_shape=jax.ShapeDtypeStruct((rows, width - 128), BF16),
        compiler_params=pltpu.CompilerParams(vmem_limit_bytes=VMEM_LIMIT),
        cost_estimate=SMALL,
        name="merge",
    )(*parts)


def flip(x, bits):
    return lax.ppermute(x, "ctx", [(i, i ^ bits) for i in range(16)])


def turn(x, k):
    return lax.ppermute(x, "ctx", [(i, (i + 4 * k) % 16) for i in range(16)])


def body(
    tokens, kv_weight, queries, cache_keys, cache_values, cache_lengths, page_owner, page_slot
):
    order = (1, 3, 2)
    others = [turn(queries, k) for k in order]
    own_kv = jnp.concatenate([cache_keys, cache_values], axis=1)
    far_kv = flip(own_kv, 2)
    core_kv = flip(own_kv, 1)

    partial = project(tokens, kv_weight)
    gathered = lax.all_to_all(partial, "tp", 0, 0, tiled=True)

    near, far = (0, 1), (2, 3)
    lengths, _ = lax.optimization_barrier((cache_lengths, partial))
    near0, near1 = attend(
        lengths, [queries, others[0]], (own_kv, core_kv), near, flops=2 * 10**10
    )
    lengths, gathered, far_kv, _ = lax.optimization_barrier((lengths, gathered, far_kv, near0))
    fresh = jnp.sum(gathered.astype(F32), axis=0).astype(BF16)
    fresh = lax.all_gather(fresh, "ctx", axis=0, tiled=True)
    both_kv = flip(far_kv, 1)
    near2, near3 = attend(lengths, others[1:], (own_kv, core_kv), near, flops=2 * 10**10)
    sent = attend(
        lengths, others, (far_kv, both_kv), far, state=[near1, near2, near3], flops=2 * 10**10
    )
    back = [turn(part, 4 - k) for part, k in zip(sent, order)]
    lengths, _ = lax.optimization_barrier((lengths, sent[0]))
    mine, kv_pages = attend(
        lengths, [queries], (far_kv, both_kv), far, state=[near0], fresh=fresh,
        pages=(page_owner, page_slot),
    )
    attended = merge([mine, *back])
    return (attended, kv_pages)


def solution(mesh):
    placed = (
        P("ctx", "tp"),
        P("tp", None),
        P("ctx", "tp"),
        P("ctx", "tp"),
        P("ctx", "tp"),
        P(),
        P(),
        P(),
    )
    return jax.shard_map(
        body,
        mesh=mesh,
        in_specs=placed,
        out_specs=(P("ctx", "tp"), P("ctx", "tp")),
        check_vma=False,
    )
```

```python
import functools

import jax
import jax.numpy as jnp
from jax import lax
from jax.experimental import pallas as pl
from jax.experimental.pallas import tpu as pltpu
from jax.sharding import PartitionSpec as P

PAGE = 32
HD = 128
LOG2E = 1.4426950408889634
SCALE = LOG2E / HD**0.5
BIG = 2.0**100
F32 = jnp.float32
BF16 = jnp.bfloat16
VMEM_LIMIT = 63 * 2**20 + 2**19 + 2**18 + 2**17
SMALL = pl.CostEstimate(flops=1000, bytes_accessed=1000, transcendentals=0)


def nt_dot(a, b):
    return lax.dot_general(a, b, (((1,), (1,)), ((), ())), preferred_element_type=F32)


def nn_dot(a, b):
    return lax.dot_general(a, b, (((1,), (0,)), ((), ())), preferred_element_type=F32)


def vmem_spec():
    return pl.BlockSpec(memory_space=pltpu.VMEM)


def smem_spec():
    return pl.BlockSpec(memory_space=pltpu.SMEM)


def project_kernel(tok_ref, w_ref, out_ref):
    result = nn_dot(tok_ref[...], w_ref[...]).astype(BF16)
    for h in range(out_ref.shape[0]):
        out_ref[h] = result[:, h * 2 * HD : (h + 1) * 2 * HD]


def project(tokens, kv_weight):
    rows, depth = tokens.shape
    heads = kv_weight.shape[1] // (2 * HD)
    at_once = 2
    return pl.pallas_call(
        project_kernel,
        grid=(heads // at_once,),
        in_specs=[
            pl.BlockSpec((rows, depth), lambda h: (0, 0)),
            pl.BlockSpec((depth, at_once * 2 * HD), lambda h: (0, h)),
        ],
        out_specs=pl.BlockSpec((at_once, rows, 2 * HD), lambda h: (h, 0, 0)),
        out_shape=jax.ShapeDtypeStruct((heads, rows, 2 * HD), BF16),
        compiler_params=pltpu.CompilerParams(vmem_limit_bytes=VMEM_LIMIT),
        cost_estimate=SMALL,
        name="project",
    )(tokens, kv_weight)


def attend_kernel(cfg, *refs):
    nq, nseg, seg, owner_xor, state_in, fresh, relay = cfg
    refs = list(refs)
    take = lambda n: [refs.pop(0) for _ in range(n)]
    (len_ref,) = take(1)
    q_refs = take(nq)
    kv_refs = take(nseg)
    f_refs = take(1) if fresh else []
    page_refs = take(2) if fresh else []
    part_refs = take(1) if relay else []
    st_refs = take(nq) if state_in else []
    outs = take(nq)
    pages_out = take(1) if fresh else []
    spread_out = take(1) if relay else []
    if relay:
        parts, total_rows, part_sem, spread_sems = refs[-4:]
        refs = refs[:-4]
    qs, qb, kb, acc, ll, mm, st, sems, q_sems, st_sems = refs
    me = lax.axis_index("ctx")
    step = pl.program_id(0)
    rows = qb.shape[0]
    groups = rows // 128
    nsegs = nseg + len(f_refs)

    copies = [
        pltpu.make_async_copy(r, kb.at[pl.ds(s * seg, seg)], sems.at[s])
        for s, r in enumerate(kv_refs + f_refs)
    ]

    q_copies = [
        pltpu.make_async_copy(r, qs.at[i], q_sems.at[i]) for i, r in enumerate(q_refs)
    ]
    st_copies = [
        pltpu.make_async_copy(r, st.at[i], st_sems.at[i]) for i, r in enumerate(st_refs)
    ]

    if relay:
        part_copy = pltpu.make_async_copy(part_refs[0], parts, part_sem.at[0])
        spread_copies = [
            pltpu.make_async_copy(total_rows, spread_out[0].at[i], spread_sems.at[i])
            for i in range(spread_out[0].shape[0])
        ]

    @pl.when(step == 0)
    def _():
        if relay:
            part_copy.start()
        q_copies[0].start()
        for c in copies[:1] + q_copies[1:] + st_copies + copies[1:]:
            c.start()

    for i in range(nq):

        @pl.when(step == i)
        def _():
            q_copies[i].wait()
            if state_in:
                st_copies[i].wait()

    for g in range(groups):
        qb[g * 128 : (g + 1) * 128, :] = qs[step, :, g * 128 : (g + 1) * 128]

    @pl.when(step == 0)
    def _():
        copies[0].wait()

    if state_in:
        side_in = st[step, :, groups * 128 :].astype(F32)
        for g in range(groups):
            mm[g * 128 : (g + 1) * 128, :] = jnp.broadcast_to(side_in[:, g : g + 1], (128, 128))
    else:
        top = jnp.max(nt_dot(qb[...], kb[:256, :HD]), axis=-1, keepdims=True) * SCALE
        mm[...] = jnp.broadcast_to(top.astype(BF16).astype(F32), mm.shape)

    if relay:

        @pl.when(step == 0)
        def _():
            part_copy.wait()
            added = parts[0].astype(F32)
            for i in range(1, parts.shape[0]):
                added = added + parts[i].astype(F32)
            total_rows[...] = added.astype(BF16)
            for c in spread_copies:
                c.start()

    def masked(vals, size, limit, slope, fill):
        col = lax.broadcasted_iota(jnp.int32, (rows, size), 1)
        row = lax.rem(lax.broadcasted_iota(jnp.int32, (rows, size), 0), 128)
        return jnp.where(col <= limit + row * slope, vals, fill)

    def accumulate(at, size, limit=None, slope=None):
        at = pl.ds(pl.multiple_of(at, 128), size)
        s = nt_dot(qb[...], kb[at, :HD])
        tops = jnp.concatenate([mm[...]] * (size // 128), axis=1)
        p = jnp.exp2(s * SCALE - tops)
        if limit is not None:
            p = masked(p, size, limit, slope, 0.0)
        acc[...] += nn_dot(p.astype(BF16), kb[at, HD:])
        total = ll[...]
        for g in range(size // 128):
            total = total + p[:, g * 128 : (g + 1) * 128]
        ll[...] = total

    def segment(s):
        owner = me ^ owner_xor[0]
        for i in range(1, nseg):
            owner = jnp.where(s == i, me ^ owner_xor[i], owner)
        length = jnp.clip(len_ref[owner], 0, seg)
        whole = length // 512 * 512
        rest = length - whole
        limit = rest - 1
        slope = 0
        if fresh:
            is_fresh = s == nseg
            before = me * 128
            whole = jnp.where(is_fresh, before // 512 * 512, whole)
            rest = jnp.where(is_fresh, before - whole + 128, rest)
            limit = jnp.where(is_fresh, before - whole, limit)
            slope = jnp.where(is_fresh, 1, 0)
        return s * seg, whole, rest, limit, slope

    def sweep(turn):
        acc[...] = jnp.zeros_like(acc)
        ll[...] = jnp.zeros_like(ll)

        def one(s, carry):
            start, whole, rest, limit, slope = segment(s)

            for i in range(1, nsegs):

                @pl.when((s == i) & (step == 0) & (turn == 0))
                def _():
                    copies[i].wait()

            wide = whole // 1024

            def wide_step(j, c):
                accumulate(start + j * 1024, 1024)
                return c

            lax.fori_loop(0, wide, wide_step, 0)

            @pl.when(whole > wide * 1024)
            def _():
                accumulate(start + wide * 1024, 512)

            @pl.when(rest > 256)
            def _():
                accumulate(start + whole, 512, limit, slope)

            @pl.when((rest > 0) & (rest <= 256))
            def _():
                accumulate(start + whole, 256, limit, slope)

            return carry

        lax.fori_loop(0, nsegs, one, 0)

    def raise_tops():
        def one(s, carry):
            start, whole, rest, limit, slope = segment(s)

            def part(j, c):
                at = pl.ds(pl.multiple_of(start + j * 128, 128), 128)
                s_now = nt_dot(qb[...], kb[at, :HD]) * SCALE
                edge = jnp.where(j * 128 < whole, 128, limit - (j * 128 - whole))
                tilt = jnp.where(j * 128 < whole, 0, slope)
                s_now = masked(s_now, 128, edge, tilt, -3.0e38)
                top = jnp.max(s_now, axis=-1, keepdims=True)
                mm[...] = jnp.maximum(mm[...], top.astype(BF16).astype(F32))
                return c

            return lax.fori_loop(0, (whole + rest + 127) // 128, part, carry)

        lax.fori_loop(0, nsegs, one, 0)

    def attempt(turn):
        @pl.when(turn == 1)
        def _():
            raise_tops()

        sweep(turn)
        fits = jnp.max(ll[...]) < BIG
        return jnp.where((turn == 0) & jnp.logical_not(fits), 1, 2)

    lax.while_loop(lambda turn: turn < 2, attempt, 0)

    lane = lax.broadcasted_iota(jnp.int32, (128, 128), 1)

    def finish(out):
        side = jnp.zeros((128, 128), F32)
        for g in range(groups):
            part = slice(g * 128, (g + 1) * 128)
            mixed = acc[part, :]
            total = jnp.sum(ll[part, :], axis=-1, keepdims=True)
            top = mm[part, :]
            if state_in:
                decay = jnp.exp2(side_in[:, g : g + 1] - top)
                mixed = mixed + st[step, :, part].astype(F32) * decay
                total = total + (side_in[:, 8 + g : 9 + g] + side_in[:, 16 + g : 17 + g]) * decay
            out[:, part] = mixed.astype(BF16)
            high = total.astype(BF16).astype(F32)
            side = jnp.where(lane == g, top, side)
            side = jnp.where(lane == 8 + g, high, side)
            side = jnp.where(lane == 16 + g, total - high, side)
        out[:, groups * 128 :] = side.astype(BF16)

    for i in range(nq):

        @pl.when(step == i)
        def _():
            finish(outs[i])

    if fresh:
        owner_ref, slot_ref = page_refs
        (pages,) = pages_out
        pages[...] = jnp.zeros_like(pages)

        def one_page(page, carry):
            @pl.when(owner_ref[page] == me)
            def _():
                src = pl.ds(pl.multiple_of(nseg * seg + page * PAGE, PAGE), PAGE)
                dst = pl.ds(pl.multiple_of(slot_ref[page] * PAGE, PAGE), PAGE)
                pages[dst, :] = kb[src, :]

            return carry

        lax.fori_loop(0, owner_ref.shape[0], one_page, 0)

    if relay:

        @pl.when(step == nq - 1)
        def _():
            for c in spread_copies:
                c.wait()


def attend(lengths, qs, kvs, owner_xor, state=None, fresh=None, pages=None, parts=None):
    nq, nseg, seg = len(qs), len(kvs), kvs[0].shape[0]
    width = qs[0].shape[1]
    rows = width
    cfg = (nq, nseg, seg, owner_xor, state is not None, fresh is not None, parts is not None)
    any_spec = pl.BlockSpec(memory_space=pl.ANY)
    args = [lengths, *qs, *kvs]
    in_specs = [smem_spec()] + [any_spec] * (nq + nseg)
    out_specs = [pl.BlockSpec((128, width + 128), lambda i: (0, 0))] * nq
    out_shape = [jax.ShapeDtypeStruct((128, width + 128), BF16)] * nq
    if fresh is not None:
        args += [fresh, *pages]
        in_specs += [any_spec, smem_spec(), smem_spec()]
        out_specs.append(pl.BlockSpec((8 * PAGE, 2 * HD), lambda i: (0, 0)))
        out_shape.append(jax.ShapeDtypeStruct((8 * PAGE, 2 * HD), BF16))
    scratch = []
    if parts is not None:
        args.append(parts)
        in_specs.append(any_spec)
        block = parts.shape[1:]
        out_specs.append(any_spec)
        out_shape.append(jax.ShapeDtypeStruct((16, *block), BF16))
        scratch = [
            pltpu.VMEM(parts.shape, BF16),
            pltpu.VMEM(block, BF16),
            pltpu.SemaphoreType.DMA((1,)),
            pltpu.SemaphoreType.DMA((16,)),
        ]
    if state is not None:
        args += state
        in_specs += [any_spec] * nq
    nsegs = nseg + (fresh is not None)
    return pl.pallas_call(
        functools.partial(attend_kernel, cfg),
        grid=(nq,),
        in_specs=in_specs,
        out_specs=out_specs,
        out_shape=out_shape,
        scratch_shapes=[
            pltpu.VMEM((nq, 128, width), BF16),
            pltpu.VMEM((rows, HD), BF16),
            pltpu.VMEM((nsegs * seg, 2 * HD), BF16),
            pltpu.VMEM((rows, HD), F32),
            pltpu.VMEM((rows, HD), F32),
            pltpu.VMEM((rows, HD), F32),
            pltpu.VMEM((nq, 128, width + 128), BF16),
            pltpu.SemaphoreType.DMA((nsegs,)),
            pltpu.SemaphoreType.DMA((nq,)),
            pltpu.SemaphoreType.DMA((nq,)),
            *scratch,
        ],
        compiler_params=pltpu.CompilerParams(vmem_limit_bytes=VMEM_LIMIT),
        cost_estimate=pl.CostEstimate(
            flops=2 * 10**10, bytes_accessed=1000, transcendentals=0
        ),
        name="attend",
    )(*args)


def merge_kernel(*refs):
    parts, out = refs[:-1], refs[-1]
    groups = out.shape[1] // 128
    sides = [r[:, groups * 128 :].astype(F32) for r in parts]
    top = functools.reduce(jnp.maximum, sides)
    scales = [jnp.exp2(s - top) for s in sides]
    total = jnp.zeros_like(top)
    for w, s in zip(scales, sides):
        total = total + w * (pltpu.roll(s, 120, 1) + pltpu.roll(s, 112, 1))
    scales = [w / total for w in scales]
    for g in range(groups):
        part = slice(g * 128, (g + 1) * 128)
        mixed = sum(w[:, g : g + 1] * r[:, part].astype(F32) for w, r in zip(scales, parts))
        out[:, part] = mixed.astype(BF16)


def merge(parts):
    rows, width = parts[0].shape
    return pl.pallas_call(
        merge_kernel,
        grid=(2,),
        in_specs=[pl.BlockSpec((rows // 2, width), lambda i: (i, 0))] * len(parts),
        out_specs=pl.BlockSpec((rows // 2, width - 128), lambda i: (i, 0)),
        out_shape=jax.ShapeDtypeStruct((rows, width - 128), BF16),
        compiler_params=pltpu.CompilerParams(vmem_limit_bytes=VMEM_LIMIT),
        cost_estimate=SMALL,
        name="merge",
    )(*parts)


def pack_kernel(k_ref, v_ref, out_ref, sems):
    copies = [
        pltpu.make_async_copy(r, out_ref.at[:, pl.ds(i * HD, HD)], sems.at[i])
        for i, r in enumerate((k_ref, v_ref))
    ]
    for c in copies:
        c.start()
    for c in copies:
        c.wait()


def pack(keys, values):
    any_spec = pl.BlockSpec(memory_space=pl.ANY)
    return pl.pallas_call(
        pack_kernel,
        in_specs=[any_spec] * 2,
        out_specs=any_spec,
        out_shape=jax.ShapeDtypeStruct((keys.shape[0], 2 * HD), BF16),
        scratch_shapes=[pltpu.SemaphoreType.DMA((2,))],
        compiler_params=pltpu.CompilerParams(vmem_limit_bytes=VMEM_LIMIT),
        cost_estimate=SMALL,
        name="pack",
    )(keys, values)


def flip(x, bits):
    return lax.ppermute(x, "ctx", [(i, i ^ bits) for i in range(16)])


def turn(x, k):
    return lax.ppermute(x, "ctx", [(i, (i + 4 * k) % 16) for i in range(16)])


def body(
    tokens, kv_weight, queries, cache_keys, cache_values, cache_lengths, page_owner, page_slot
):
    order = (1, 3, 2)
    others = [turn(queries, k) for k in order]
    own_kv = pack(cache_keys, cache_values)
    far_kv = flip(own_kv, 2)
    core_kv = flip(own_kv, 1)

    partial = project(tokens, kv_weight)
    gathered = lax.all_to_all(partial, "tp", 0, 0, tiled=True)

    near, far = (0, 1), (2, 3)
    lengths, _ = lax.optimization_barrier((cache_lengths, partial))
    near1, near2 = attend(lengths, others[:2], (own_kv, core_kv), near)
    lengths, gathered, far_kv, _ = lax.optimization_barrier((lengths, gathered, far_kv, near1))
    both_kv = flip(far_kv, 1)
    near3, spread = attend(lengths, others[2:], (own_kv, core_kv), near, parts=gathered)
    fresh = lax.all_to_all(spread, "ctx", 0, 0, tiled=True).reshape(16 * 128, 2 * HD)
    sent = attend(lengths, others, (far_kv, both_kv), far, state=[near1, near2, near3])
    back = [turn(part, 4 - k) for part, k in zip(sent, order)]
    lengths, _ = lax.optimization_barrier((lengths, sent[0]))
    mine, kv_pages = attend(
        lengths, [queries], (own_kv, core_kv, far_kv, both_kv), near + far, fresh=fresh,
        pages=(page_owner, page_slot),
    )
    attended = merge([mine, *back])
    return (attended, kv_pages)


def solution(mesh):
    placed = (
        P("ctx", "tp"),
        P("tp", None),
        P("ctx", "tp"),
        P("ctx", "tp"),
        P("ctx", "tp"),
        P(),
        P(),
        P(),
    )
    return jax.shard_map(
        body,
        mesh=mesh,
        in_specs=placed,
        out_specs=(P("ctx", "tp"), P("ctx", "tp")),
        check_vma=False,
    )
```

```python
import functools

import jax
import jax.numpy as jnp
from jax import lax
from jax.experimental import pallas as pl
from jax.experimental.pallas import tpu as pltpu
from jax.sharding import PartitionSpec as P

PAGE = 32
HD = 128
LOG2E = 1.4426950408889634
SCALE = LOG2E / HD**0.5
BIG = 2.0**100
F32 = jnp.float32
BF16 = jnp.bfloat16
VMEM_LIMIT = 63 * 2**20 + 2**19 + 2**18 + 2**17
SMALL = pl.CostEstimate(flops=1000, bytes_accessed=1000, transcendentals=0)


def nt_dot(a, b):
    return lax.dot_general(a, b, (((1,), (1,)), ((), ())), preferred_element_type=F32)


def nn_dot(a, b):
    return lax.dot_general(a, b, (((1,), (0,)), ((), ())), preferred_element_type=F32)


def vmem_spec():
    return pl.BlockSpec(memory_space=pltpu.VMEM)


def smem_spec():
    return pl.BlockSpec(memory_space=pltpu.SMEM)


def project_kernel(tok_ref, w_ref, out_ref):
    result = nn_dot(tok_ref[...], w_ref[...]).astype(BF16)
    for h in range(out_ref.shape[0]):
        out_ref[h] = result[:, h * 2 * HD : (h + 1) * 2 * HD]


def project(tokens, kv_weight):
    rows, depth = tokens.shape
    heads = kv_weight.shape[1] // (2 * HD)
    at_once = 2
    return pl.pallas_call(
        project_kernel,
        grid=(heads // at_once,),
        in_specs=[
            pl.BlockSpec((rows, depth), lambda h: (0, 0)),
            pl.BlockSpec((depth, at_once * 2 * HD), lambda h: (0, h)),
        ],
        out_specs=pl.BlockSpec((at_once, rows, 2 * HD), lambda h: (h, 0, 0)),
        out_shape=jax.ShapeDtypeStruct((heads, rows, 2 * HD), BF16),
        compiler_params=pltpu.CompilerParams(vmem_limit_bytes=VMEM_LIMIT),
        cost_estimate=SMALL,
        name="project",
    )(tokens, kv_weight)


def attend_kernel(cfg, *refs):
    nq, nseg, seg, owner_xor, state_in, fresh, relay = cfg
    refs = list(refs)
    take = lambda n: [refs.pop(0) for _ in range(n)]
    (len_ref,) = take(1)
    q_refs = take(nq)
    kv_refs = take(nseg)
    f_refs = take(1) if fresh else []
    page_refs = take(2) if fresh else []
    part_refs = take(1) if relay else []
    st_refs = take(nq) if state_in else []
    outs = take(nq)
    pages_out = take(1) if fresh else []
    spread_out = take(1) if relay else []
    if relay:
        parts, total_rows, part_sem, spread_sems = refs[-4:]
        refs = refs[:-4]
    qs, qb, kb, acc, ll, mm, st, sems, q_sems, st_sems = refs
    me = lax.axis_index("ctx")
    rows = qb.shape[0]
    groups = qs.shape[2] // 128
    nsegs = nseg + len(f_refs)

    copies = [
        pltpu.make_async_copy(r, kb.at[pl.ds(s * seg, seg)], sems.at[s])
        for s, r in enumerate(kv_refs + f_refs)
    ]

    q_copies = [
        pltpu.make_async_copy(r, qs.at[i], q_sems.at[i]) for i, r in enumerate(q_refs)
    ]
    st_copies = [
        pltpu.make_async_copy(r, st.at[i], st_sems.at[i]) for i, r in enumerate(st_refs)
    ]

    if relay:
        part_copy = pltpu.make_async_copy(part_refs[0], parts, part_sem.at[0])
        spread_copies = [
            pltpu.make_async_copy(total_rows, spread_out[0].at[i], spread_sems.at[i])
            for i in range(spread_out[0].shape[0])
        ]

    if relay:
        part_copy.start()
    q_copies[0].start()
    for c in copies[:1] + q_copies[1:] + st_copies + copies[1:]:
        c.start()
    for i in range(nq):
        q_copies[i].wait()
        for g in range(groups):
            at = (i * groups + g) * 128
            qb[at : at + 128, :] = qs[i, :, g * 128 : (g + 1) * 128]
    copies[0].wait()

    if state_in:
        sides = []
        for i in range(nq):
            st_copies[i].wait()
            sides.append(st[i, :, groups * 128 :].astype(F32))
            for g in range(groups):
                at = (i * groups + g) * 128
                mm[at : at + 128, :] = jnp.broadcast_to(sides[i][:, g : g + 1], (128, 128))
    else:
        top = jnp.max(nt_dot(qb[...], kb[:256, :HD]), axis=-1, keepdims=True) * SCALE
        mm[...] = jnp.broadcast_to(top.astype(BF16).astype(F32), mm.shape)

    if relay:
        part_copy.wait()
        added = parts[0].astype(F32)
        for i in range(1, parts.shape[0]):
            added = added + parts[i].astype(F32)
        total_rows[...] = added.astype(BF16)
        for c in spread_copies:
            c.start()

    def masked(vals, size, limit, slope, fill):
        col = lax.broadcasted_iota(jnp.int32, (rows, size), 1)
        row = lax.rem(lax.broadcasted_iota(jnp.int32, (rows, size), 0), 128)
        return jnp.where(col <= limit + row * slope, vals, fill)

    def accumulate(at, size, limit=None, slope=None):
        at = pl.ds(pl.multiple_of(at, 128), size)
        s = nt_dot(qb[...], kb[at, :HD])
        tops = jnp.concatenate([mm[...]] * (size // 128), axis=1)
        p = jnp.exp2(s * SCALE - tops)
        if limit is not None:
            p = masked(p, size, limit, slope, 0.0)
        acc[...] += nn_dot(p.astype(BF16), kb[at, HD:])
        total = ll[...]
        for g in range(size // 128):
            total = total + p[:, g * 128 : (g + 1) * 128]
        ll[...] = total

    def segment(s):
        owner = me ^ owner_xor[0]
        for i in range(1, nseg):
            owner = jnp.where(s == i, me ^ owner_xor[i], owner)
        length = jnp.clip(len_ref[owner], 0, seg)
        whole = length // 512 * 512
        rest = length - whole
        limit = rest - 1
        slope = 0
        if fresh:
            is_fresh = s == nseg
            before = me * 128
            whole = jnp.where(is_fresh, before // 512 * 512, whole)
            rest = jnp.where(is_fresh, before - whole + 128, rest)
            limit = jnp.where(is_fresh, before - whole, limit)
            slope = jnp.where(is_fresh, 1, 0)
        return s * seg, whole, rest, limit, slope

    def sweep(turn):
        acc[...] = jnp.zeros_like(acc)
        ll[...] = jnp.zeros_like(ll)

        def one(s, carry):
            start, whole, rest, limit, slope = segment(s)

            for i in range(1, nsegs):

                @pl.when((s == i) & (turn == 0))
                def _():
                    copies[i].wait()

            wide = whole // 1024

            def wide_step(j, c):
                accumulate(start + j * 1024, 1024)
                return c

            lax.fori_loop(0, wide, wide_step, 0)

            @pl.when(whole > wide * 1024)
            def _():
                accumulate(start + wide * 1024, 512)

            @pl.when(rest > 256)
            def _():
                accumulate(start + whole, 512, limit, slope)

            @pl.when((rest > 0) & (rest <= 256))
            def _():
                accumulate(start + whole, 256, limit, slope)

            return carry

        lax.fori_loop(0, nsegs, one, 0)

    def raise_tops():
        def one(s, carry):
            start, whole, rest, limit, slope = segment(s)

            def part(j, c):
                at = pl.ds(pl.multiple_of(start + j * 128, 128), 128)
                s_now = nt_dot(qb[...], kb[at, :HD]) * SCALE
                edge = jnp.where(j * 128 < whole, 128, limit - (j * 128 - whole))
                tilt = jnp.where(j * 128 < whole, 0, slope)
                s_now = masked(s_now, 128, edge, tilt, -3.0e38)
                top = jnp.max(s_now, axis=-1, keepdims=True)
                mm[...] = jnp.maximum(mm[...], top.astype(BF16).astype(F32))
                return c

            return lax.fori_loop(0, (whole + rest + 127) // 128, part, carry)

        lax.fori_loop(0, nsegs, one, 0)

    def attempt(turn):
        @pl.when(turn == 1)
        def _():
            raise_tops()

        sweep(turn)
        fits = jnp.max(ll[...]) < BIG
        return jnp.where((turn == 0) & jnp.logical_not(fits), 1, 2)

    lax.while_loop(lambda turn: turn < 2, attempt, 0)

    lane = lax.broadcasted_iota(jnp.int32, (128, 128), 1)

    for i in range(nq):
        out = outs[i]
        side = jnp.zeros((128, 128), F32)
        for g in range(groups):
            rows_at = slice((i * groups + g) * 128, (i * groups + g + 1) * 128)
            part = slice(g * 128, (g + 1) * 128)
            mixed = acc[rows_at, :]
            total = jnp.sum(ll[rows_at, :], axis=-1, keepdims=True)
            top = mm[rows_at, :]
            if state_in:
                before = sides[i]
                decay = jnp.exp2(before[:, g : g + 1] - top)
                mixed = mixed + st[i, :, part].astype(F32) * decay
                total = total + (before[:, 8 + g : 9 + g] + before[:, 16 + g : 17 + g]) * decay
            out[:, part] = mixed.astype(BF16)
            high = total.astype(BF16).astype(F32)
            side = jnp.where(lane == g, top, side)
            side = jnp.where(lane == 8 + g, high, side)
            side = jnp.where(lane == 16 + g, total - high, side)
        out[:, groups * 128 :] = side.astype(BF16)

    if fresh:
        owner_ref, slot_ref = page_refs
        (pages,) = pages_out
        pages[...] = jnp.zeros_like(pages)

        def one_page(page, carry):
            @pl.when(owner_ref[page] == me)
            def _():
                src = pl.ds(pl.multiple_of(nseg * seg + page * PAGE, PAGE), PAGE)
                dst = pl.ds(pl.multiple_of(slot_ref[page] * PAGE, PAGE), PAGE)
                pages[dst, :] = kb[src, :]

            return carry

        lax.fori_loop(0, owner_ref.shape[0], one_page, 0)

    if relay:
        for c in spread_copies:
            c.wait()


def attend(lengths, qs, kvs, owner_xor, state=None, fresh=None, pages=None, parts=None):
    nq, nseg, seg = len(qs), len(kvs), kvs[0].shape[0]
    width = qs[0].shape[1]
    rows = nq * width
    cfg = (nq, nseg, seg, owner_xor, state is not None, fresh is not None, parts is not None)
    any_spec = pl.BlockSpec(memory_space=pl.ANY)
    args = [lengths, *qs, *kvs]
    in_specs = [smem_spec()] + [any_spec] * (nq + nseg)
    out_specs = [pl.BlockSpec((128, width + 128), lambda i: (0, 0))] * nq
    out_shape = [jax.ShapeDtypeStruct((128, width + 128), BF16)] * nq
    if fresh is not None:
        args += [fresh, *pages]
        in_specs += [any_spec, smem_spec(), smem_spec()]
        out_specs.append(pl.BlockSpec((8 * PAGE, 2 * HD), lambda i: (0, 0)))
        out_shape.append(jax.ShapeDtypeStruct((8 * PAGE, 2 * HD), BF16))
    scratch = []
    if parts is not None:
        args.append(parts)
        in_specs.append(any_spec)
        block = parts.shape[1:]
        out_specs.append(any_spec)
        out_shape.append(jax.ShapeDtypeStruct((16, *block), BF16))
        scratch = [
            pltpu.VMEM(parts.shape, BF16),
            pltpu.VMEM(block, BF16),
            pltpu.SemaphoreType.DMA((1,)),
            pltpu.SemaphoreType.DMA((16,)),
        ]
    if state is not None:
        args += state
        in_specs += [any_spec] * nq
    nsegs = nseg + (fresh is not None)
    return pl.pallas_call(
        functools.partial(attend_kernel, cfg),
        grid=(1,),
        in_specs=in_specs,
        out_specs=out_specs,
        out_shape=out_shape,
        scratch_shapes=[
            pltpu.VMEM((nq, 128, width), BF16),
            pltpu.VMEM((rows, HD), BF16),
            pltpu.VMEM((nsegs * seg, 2 * HD), BF16),
            pltpu.VMEM((rows, HD), F32),
            pltpu.VMEM((rows, HD), F32),
            pltpu.VMEM((rows, HD), F32),
            pltpu.VMEM((nq, 128, width + 128), BF16),
            pltpu.SemaphoreType.DMA((nsegs,)),
            pltpu.SemaphoreType.DMA((nq,)),
            pltpu.SemaphoreType.DMA((nq,)),
            *scratch,
        ],
        compiler_params=pltpu.CompilerParams(vmem_limit_bytes=VMEM_LIMIT),
        cost_estimate=pl.CostEstimate(
            flops=2 * 10**10, bytes_accessed=1000, transcendentals=0
        ),
        name="attend",
    )(*args)


def merge_kernel(*refs):
    parts, out = refs[:-1], refs[-1]
    groups = out.shape[1] // 128
    sides = [r[:, groups * 128 :].astype(F32) for r in parts]
    top = functools.reduce(jnp.maximum, sides)
    scales = [jnp.exp2(s - top) for s in sides]
    total = jnp.zeros_like(top)
    for w, s in zip(scales, sides):
        total = total + w * (pltpu.roll(s, 120, 1) + pltpu.roll(s, 112, 1))
    scales = [w / total for w in scales]
    for g in range(groups):
        part = slice(g * 128, (g + 1) * 128)
        mixed = sum(w[:, g : g + 1] * r[:, part].astype(F32) for w, r in zip(scales, parts))
        out[:, part] = mixed.astype(BF16)


def merge(parts):
    rows, width = parts[0].shape
    return pl.pallas_call(
        merge_kernel,
        grid=(2,),
        in_specs=[pl.BlockSpec((rows // 2, width), lambda i: (i, 0))] * len(parts),
        out_specs=pl.BlockSpec((rows // 2, width - 128), lambda i: (i, 0)),
        out_shape=jax.ShapeDtypeStruct((rows, width - 128), BF16),
        compiler_params=pltpu.CompilerParams(vmem_limit_bytes=VMEM_LIMIT),
        cost_estimate=SMALL,
        name="merge",
    )(*parts)


def flip(x, bits):
    return lax.ppermute(x, "ctx", [(i, i ^ bits) for i in range(16)])


def turn(x, k):
    return lax.ppermute(x, "ctx", [(i, (i + 4 * k) % 16) for i in range(16)])


def body(
    tokens, kv_weight, queries, cache_keys, cache_values, cache_lengths, page_owner, page_slot
):
    order = (1, 3, 2)
    others = [turn(queries, k) for k in order]
    own_kv = jnp.concatenate([cache_keys, cache_values], axis=1)
    far_kv = flip(own_kv, 2)
    core_kv = flip(own_kv, 1)

    partial = project(tokens, kv_weight)
    gathered = lax.all_to_all(partial, "tp", 0, 0, tiled=True)

    near, far = (0, 1), (2, 3)
    lengths, _ = lax.optimization_barrier((cache_lengths, partial))
    near1, near2 = attend(lengths, others[:2], (own_kv, core_kv), near)
    lengths, gathered, far_kv, _ = lax.optimization_barrier((lengths, gathered, far_kv, near1))
    both_kv = flip(far_kv, 1)
    near3, spread = attend(lengths, others[2:], (own_kv, core_kv), near, parts=gathered)
    fresh = lax.all_to_all(spread, "ctx", 0, 0, tiled=True).reshape(16 * 128, 2 * HD)
    sent = attend(lengths, others, (far_kv, both_kv), far, state=[near1, near2, near3])
    back = [turn(part, 4 - k) for part, k in zip(sent, order)]
    lengths, _ = lax.optimization_barrier((lengths, sent[0]))
    mine, kv_pages = attend(
        lengths, [queries], (own_kv, core_kv, far_kv, both_kv), near + far, fresh=fresh,
        pages=(page_owner, page_slot),
    )
    attended = merge([mine, *back])
    return (attended, kv_pages)


def solution(mesh):
    placed = (
        P("ctx", "tp"),
        P("tp", None),
        P("ctx", "tp"),
        P("ctx", "tp"),
        P("ctx", "tp"),
        P(),
        P(),
        P(),
    )
    return jax.shard_map(
        body,
        mesh=mesh,
        in_specs=placed,
        out_specs=(P("ctx", "tp"), P("ctx", "tp")),
        check_vma=False,
    )
```

```python
import functools

import jax
import jax.numpy as jnp
from jax import lax
from jax.experimental import pallas as pl
from jax.experimental.pallas import tpu as pltpu
from jax.sharding import PartitionSpec as P

PAGE = 32
HD = 128
LOG2E = 1.4426950408889634
SCALE = LOG2E / HD**0.5
BIG = 2.0**100
F32 = jnp.float32
BF16 = jnp.bfloat16
FIRST = 4 * 10**9
VMEM_LIMIT = 63 * 2**20 + 2**19 + 2**18 + 2**17
SMALL = pl.CostEstimate(flops=1000, bytes_accessed=1000, transcendentals=0)


def nt_dot(a, b):
    return lax.dot_general(a, b, (((1,), (1,)), ((), ())), preferred_element_type=F32)


def nn_dot(a, b):
    return lax.dot_general(a, b, (((1,), (0,)), ((), ())), preferred_element_type=F32)


def vmem_spec():
    return pl.BlockSpec(memory_space=pltpu.VMEM)


def smem_spec():
    return pl.BlockSpec(memory_space=pltpu.SMEM)


def project_kernel(tok_ref, w_ref, out_ref):
    result = nn_dot(tok_ref[...], w_ref[...]).astype(BF16)
    for h in range(out_ref.shape[0]):
        out_ref[h] = result[:, h * 2 * HD : (h + 1) * 2 * HD]


def project(tokens, kv_weight):
    rows, depth = tokens.shape
    heads = kv_weight.shape[1] // (2 * HD)
    at_once = 2
    return pl.pallas_call(
        project_kernel,
        grid=(heads // at_once,),
        in_specs=[
            pl.BlockSpec((rows, depth), lambda h: (0, 0)),
            pl.BlockSpec((depth, at_once * 2 * HD), lambda h: (0, h)),
        ],
        out_specs=pl.BlockSpec((at_once, rows, 2 * HD), lambda h: (h, 0, 0)),
        out_shape=jax.ShapeDtypeStruct((heads, rows, 2 * HD), BF16),
        compiler_params=pltpu.CompilerParams(vmem_limit_bytes=VMEM_LIMIT),
        cost_estimate=SMALL,
        name="project",
    )(tokens, kv_weight)


def attend_kernel(cfg, *refs):
    nq, nseg, seg, owner_xor, state_in, fresh = cfg
    refs = list(refs)
    take = lambda n: [refs.pop(0) for _ in range(n)]
    (len_ref,) = take(1)
    q_refs = take(nq)
    kv_refs = take(nseg)
    f_refs = take(1) if fresh else []
    page_refs = take(2) if fresh else []
    st_refs = take(nq) if state_in else []
    outs = take(nq)
    pages_out = take(1) if fresh else []
    qs, qb, kb, acc, ll, mm, st, sems, q_sems, st_sems = refs
    me = lax.axis_index("ctx")
    rows = qb.shape[0]
    groups = qs.shape[2] // 128
    nsegs = nseg + len(f_refs)

    copies = [
        pltpu.make_async_copy(r, kb.at[pl.ds(s * seg, seg)], sems.at[s])
        for s, r in enumerate(kv_refs + f_refs)
    ]

    q_copies = [
        pltpu.make_async_copy(r, qs.at[i], q_sems.at[i]) for i, r in enumerate(q_refs)
    ]
    st_copies = [
        pltpu.make_async_copy(r, st.at[i], st_sems.at[i]) for i, r in enumerate(st_refs)
    ]

    q_copies[0].start()
    for c in copies[:1] + q_copies[1:] + st_copies + copies[1:]:
        c.start()
    for i in range(nq):
        q_copies[i].wait()
        for g in range(groups):
            at = (i * groups + g) * 128
            qb[at : at + 128, :] = qs[i, :, g * 128 : (g + 1) * 128]
    copies[0].wait()

    if state_in:
        sides = []
        for i in range(nq):
            st_copies[i].wait()
            sides.append(st[i, :, groups * 128 :].astype(F32))
            for g in range(groups):
                at = (i * groups + g) * 128
                mm[at : at + 128, :] = jnp.broadcast_to(sides[i][:, g : g + 1], (128, 128))
    else:
        top = jnp.max(nt_dot(qb[...], kb[:256, :HD]), axis=-1, keepdims=True) * SCALE
        mm[...] = jnp.broadcast_to(top.astype(BF16).astype(F32), mm.shape)

    def masked(vals, size, limit, slope, fill):
        col = lax.broadcasted_iota(jnp.int32, (rows, size), 1)
        row = lax.rem(lax.broadcasted_iota(jnp.int32, (rows, size), 0), 128)
        return jnp.where(col <= limit + row * slope, vals, fill)

    def accumulate(at, size, limit=None, slope=None):
        at = pl.ds(pl.multiple_of(at, 128), size)
        s = nt_dot(qb[...], kb[at, :HD])
        tops = jnp.concatenate([mm[...]] * (size // 128), axis=1)
        p = jnp.exp2(s * SCALE - tops)
        if limit is not None:
            p = masked(p, size, limit, slope, 0.0)
        acc[...] += nn_dot(p.astype(BF16), kb[at, HD:])
        total = ll[...]
        for g in range(size // 128):
            total = total + p[:, g * 128 : (g + 1) * 128]
        ll[...] = total

    def segment(s):
        owner = me ^ owner_xor[0]
        for i in range(1, nseg):
            owner = jnp.where(s == i, me ^ owner_xor[i], owner)
        length = jnp.clip(len_ref[owner], 0, seg)
        whole = length // 512 * 512
        rest = length - whole
        limit = rest - 1
        slope = 0
        if fresh:
            is_fresh = s == nseg
            before = me * 128
            whole = jnp.where(is_fresh, before // 512 * 512, whole)
            rest = jnp.where(is_fresh, before - whole + 128, rest)
            limit = jnp.where(is_fresh, before - whole, limit)
            slope = jnp.where(is_fresh, 1, 0)
        return s * seg, whole, rest, limit, slope

    def sweep(turn):
        acc[...] = jnp.zeros_like(acc)
        ll[...] = jnp.zeros_like(ll)

        def one(s, carry):
            start, whole, rest, limit, slope = segment(s)

            for i in range(1, nsegs):

                @pl.when((s == i) & (turn == 0))
                def _():
                    copies[i].wait()

            wide = whole // 1024

            def wide_step(j, c):
                accumulate(start + j * 1024, 1024)
                return c

            lax.fori_loop(0, wide, wide_step, 0)

            @pl.when(whole > wide * 1024)
            def _():
                accumulate(start + wide * 1024, 512)

            @pl.when(rest > 256)
            def _():
                accumulate(start + whole, 512, limit, slope)

            @pl.when((rest > 0) & (rest <= 256))
            def _():
                accumulate(start + whole, 256, limit, slope)

            return carry

        lax.fori_loop(0, nsegs, one, 0)

    def raise_tops():
        def one(s, carry):
            start, whole, rest, limit, slope = segment(s)

            def part(j, c):
                at = pl.ds(pl.multiple_of(start + j * 128, 128), 128)
                s_now = nt_dot(qb[...], kb[at, :HD]) * SCALE
                edge = jnp.where(j * 128 < whole, 128, limit - (j * 128 - whole))
                tilt = jnp.where(j * 128 < whole, 0, slope)
                s_now = masked(s_now, 128, edge, tilt, -3.0e38)
                top = jnp.max(s_now, axis=-1, keepdims=True)
                mm[...] = jnp.maximum(mm[...], top.astype(BF16).astype(F32))
                return c

            return lax.fori_loop(0, (whole + rest + 127) // 128, part, carry)

        lax.fori_loop(0, nsegs, one, 0)

    def attempt(turn):
        @pl.when(turn == 1)
        def _():
            raise_tops()

        sweep(turn)
        fits = jnp.max(ll[...]) < BIG
        return jnp.where((turn == 0) & jnp.logical_not(fits), 1, 2)

    lax.while_loop(lambda turn: turn < 2, attempt, 0)

    lane = lax.broadcasted_iota(jnp.int32, (128, 128), 1)

    for i in range(nq):
        out = outs[i]
        side = jnp.zeros((128, 128), F32)
        for g in range(groups):
            rows_at = slice((i * groups + g) * 128, (i * groups + g + 1) * 128)
            part = slice(g * 128, (g + 1) * 128)
            mixed = acc[rows_at, :]
            total = jnp.sum(ll[rows_at, :], axis=-1, keepdims=True)
            top = mm[rows_at, :]
            if state_in:
                before = sides[i]
                decay = jnp.exp2(before[:, g : g + 1] - top)
                mixed = mixed + st[i, :, part].astype(F32) * decay
                total = total + (before[:, 8 + g : 9 + g] + before[:, 16 + g : 17 + g]) * decay
            out[:, part] = mixed.astype(BF16)
            high = total.astype(BF16).astype(F32)
            side = jnp.where(lane == g, top, side)
            side = jnp.where(lane == 8 + g, high, side)
            side = jnp.where(lane == 16 + g, total - high, side)
        out[:, groups * 128 :] = side.astype(BF16)

    if fresh:
        owner_ref, slot_ref = page_refs
        (pages,) = pages_out
        pages[...] = jnp.zeros_like(pages)

        def one_page(page, carry):
            @pl.when(owner_ref[page] == me)
            def _():
                src = pl.ds(pl.multiple_of(nseg * seg + page * PAGE, PAGE), PAGE)
                dst = pl.ds(pl.multiple_of(slot_ref[page] * PAGE, PAGE), PAGE)
                pages[dst, :] = kb[src, :]

            return carry

        lax.fori_loop(0, owner_ref.shape[0], one_page, 0)


def attend(
    lengths, qs, kvs, owner_xor, state=None, fresh=None, pages=None, flops=2 * 10**10
):
    nq, nseg, seg = len(qs), len(kvs), kvs[0].shape[0]
    width = qs[0].shape[1]
    rows = nq * width
    cfg = (nq, nseg, seg, owner_xor, state is not None, fresh is not None)
    any_spec = pl.BlockSpec(memory_space=pl.ANY)
    args = [lengths, *qs, *kvs]
    in_specs = [smem_spec()] + [any_spec] * (nq + nseg)
    out_specs = [pl.BlockSpec((128, width + 128), lambda i: (0, 0))] * nq
    out_shape = [jax.ShapeDtypeStruct((128, width + 128), BF16)] * nq
    if fresh is not None:
        args += [fresh, *pages]
        in_specs += [any_spec, smem_spec(), smem_spec()]
        out_specs.append(pl.BlockSpec((8 * PAGE, 2 * HD), lambda i: (0, 0)))
        out_shape.append(jax.ShapeDtypeStruct((8 * PAGE, 2 * HD), BF16))
    if state is not None:
        args += state
        in_specs += [any_spec] * nq
    nsegs = nseg + (fresh is not None)
    return pl.pallas_call(
        functools.partial(attend_kernel, cfg),
        grid=(1,),
        in_specs=in_specs,
        out_specs=out_specs,
        out_shape=out_shape,
        scratch_shapes=[
            pltpu.VMEM((nq, 128, width), BF16),
            pltpu.VMEM((rows, HD), BF16),
            pltpu.VMEM((nsegs * seg, 2 * HD), BF16),
            pltpu.VMEM((rows, HD), F32),
            pltpu.VMEM((rows, HD), F32),
            pltpu.VMEM((rows, HD), F32),
            pltpu.VMEM((nq, 128, width + 128), BF16),
            pltpu.SemaphoreType.DMA((nsegs,)),
            pltpu.SemaphoreType.DMA((nq,)),
            pltpu.SemaphoreType.DMA((nq,)),
        ],
        compiler_params=pltpu.CompilerParams(vmem_limit_bytes=VMEM_LIMIT),
        cost_estimate=pl.CostEstimate(
            flops=flops, bytes_accessed=1000, transcendentals=0
        ),
        name="attend",
    )(*args)


def merge_kernel(*refs):
    parts, out = refs[:-1], refs[-1]
    groups = out.shape[1] // 128
    sides = [r[:, groups * 128 :].astype(F32) for r in parts]
    top = functools.reduce(jnp.maximum, sides)
    scales = [jnp.exp2(s - top) for s in sides]
    total = jnp.zeros_like(top)
    for w, s in zip(scales, sides):
        total = total + w * (pltpu.roll(s, 120, 1) + pltpu.roll(s, 112, 1))
    scales = [w / total for w in scales]
    for g in range(groups):
        part = slice(g * 128, (g + 1) * 128)
        mixed = sum(w[:, g : g + 1] * r[:, part].astype(F32) for w, r in zip(scales, parts))
        out[:, part] = mixed.astype(BF16)


def merge(parts):
    rows, width = parts[0].shape
    return pl.pallas_call(
        merge_kernel,
        grid=(2,),
        in_specs=[pl.BlockSpec((rows // 2, width), lambda i: (i, 0))] * len(parts),
        out_specs=pl.BlockSpec((rows // 2, width - 128), lambda i: (i, 0)),
        out_shape=jax.ShapeDtypeStruct((rows, width - 128), BF16),
        compiler_params=pltpu.CompilerParams(vmem_limit_bytes=VMEM_LIMIT),
        cost_estimate=SMALL,
        name="merge",
    )(*parts)


def relay_kernel(parts, spread, total, sems):
    added = parts[0].astype(F32)
    for i in range(1, parts.shape[0]):
        added = added + parts[i].astype(F32)
    total[...] = added.astype(BF16)
    copies = [
        pltpu.make_async_copy(total, spread.at[i], sems.at[i]) for i in range(spread.shape[0])
    ]
    for c in copies:
        c.start()
    for c in copies:
        c.wait()


def relay(parts, count):
    block = parts.shape[1:]
    return pl.pallas_call(
        relay_kernel,
        in_specs=[vmem_spec()],
        out_specs=pl.BlockSpec(memory_space=pl.ANY),
        out_shape=jax.ShapeDtypeStruct((count, *block), BF16),
        scratch_shapes=[pltpu.VMEM(block, BF16), pltpu.SemaphoreType.DMA((count,))],
        compiler_params=pltpu.CompilerParams(vmem_limit_bytes=VMEM_LIMIT),
        cost_estimate=pl.CostEstimate(
            flops=2 * 10**10, bytes_accessed=1000, transcendentals=0
        ),
        name="relay",
    )(parts)


def flip(x, bits):
    return lax.ppermute(x, "ctx", [(i, i ^ bits) for i in range(16)])


def turn(x, k):
    return lax.ppermute(x, "ctx", [(i, (i + 4 * k) % 16) for i in range(16)])


def body(
    tokens, kv_weight, queries, cache_keys, cache_values, cache_lengths, page_owner, page_slot
):
    order = (1, 3, 2)
    others = [turn(queries, k) for k in order]
    own_kv = jnp.concatenate([cache_keys, cache_values], axis=1)
    far_kv = flip(own_kv, 2)
    core_kv = flip(own_kv, 1)

    partial = project(tokens, kv_weight)
    gathered = lax.all_to_all(partial, "tp", 0, 0, tiled=True)

    near, far = (0, 1), (2, 3)
    lengths, _ = lax.optimization_barrier((cache_lengths, partial))
    nears = attend(lengths, others, (own_kv, core_kv), near, flops=FIRST)
    lengths, gathered, far_kv, _ = lax.optimization_barrier((lengths, gathered, far_kv, nears[0]))
    both_kv = flip(far_kv, 1)
    spread = relay(gathered, 16)
    fresh = lax.all_to_all(spread, "ctx", 0, 0, tiled=True).reshape(16 * 128, 2 * HD)
    sent = attend(lengths, others, (far_kv, both_kv), far, state=list(nears))
    back = [turn(part, 4 - k) for part, k in zip(sent, order)]
    lengths, _ = lax.optimization_barrier((lengths, sent[0]))
    mine, kv_pages = attend(
        lengths, [queries], (own_kv, core_kv, far_kv, both_kv), near + far, fresh=fresh,
        pages=(page_owner, page_slot),
    )
    attended = merge([mine, *back])
    return (attended, kv_pages)


def solution(mesh):
    placed = (
        P("ctx", "tp"),
        P("tp", None),
        P("ctx", "tp"),
        P("ctx", "tp"),
        P("ctx", "tp"),
        P(),
        P(),
        P(),
    )
    return jax.shard_map(
        body,
        mesh=mesh,
        in_specs=placed,
        out_specs=(P("ctx", "tp"), P("ctx", "tp")),
        check_vma=False,
    )
```

```python
import functools

import jax
import jax.numpy as jnp
from jax import lax
from jax.experimental import pallas as pl
from jax.experimental.pallas import tpu as pltpu
from jax.sharding import PartitionSpec as P

PAGE = 32
HD = 128
LOG2E = 1.4426950408889634
SCALE = LOG2E / HD**0.5
BIG = 2.0**100
F32 = jnp.float32
BF16 = jnp.bfloat16
FIRST = 4 * 10**9
VMEM_LIMIT = 63 * 2**20 + 2**19 + 2**18 + 2**17
SMALL = pl.CostEstimate(flops=1000, bytes_accessed=1000, transcendentals=0)


def nt_dot(a, b):
    return lax.dot_general(a, b, (((1,), (1,)), ((), ())), preferred_element_type=F32)


def nn_dot(a, b):
    return lax.dot_general(a, b, (((1,), (0,)), ((), ())), preferred_element_type=F32)


def vmem_spec():
    return pl.BlockSpec(memory_space=pltpu.VMEM)


def smem_spec():
    return pl.BlockSpec(memory_space=pltpu.SMEM)


def project_kernel(tok_ref, w_ref, out_ref):
    result = nn_dot(tok_ref[...], w_ref[...]).astype(BF16)
    for h in range(out_ref.shape[0]):
        out_ref[h] = result[:, h * 2 * HD : (h + 1) * 2 * HD]


def project(tokens, kv_weight):
    rows, depth = tokens.shape
    heads = kv_weight.shape[1] // (2 * HD)
    at_once = 4
    return pl.pallas_call(
        project_kernel,
        grid=(heads // at_once,),
        in_specs=[
            pl.BlockSpec((rows, depth), lambda h: (0, 0)),
            pl.BlockSpec((depth, at_once * 2 * HD), lambda h: (0, h)),
        ],
        out_specs=pl.BlockSpec((at_once, rows, 2 * HD), lambda h: (h, 0, 0)),
        out_shape=jax.ShapeDtypeStruct((heads, rows, 2 * HD), BF16),
        compiler_params=pltpu.CompilerParams(vmem_limit_bytes=VMEM_LIMIT),
        cost_estimate=SMALL,
        name="project",
    )(tokens, kv_weight)


def attend_kernel(cfg, *refs):
    nq, nseg, seg, owner_xor, state_in, fresh = cfg
    refs = list(refs)
    take = lambda n: [refs.pop(0) for _ in range(n)]
    (len_ref,) = take(1)
    q_refs = take(nq)
    kv_refs = take(nseg)
    f_refs = take(1) if fresh else []
    page_refs = take(2) if fresh else []
    st_refs = take(nq) if state_in else []
    outs = take(nq)
    pages_out = take(1) if fresh else []
    qs, qb, kb, acc, ll, mm, st, sems, q_sems, st_sems = refs
    me = lax.axis_index("ctx")
    rows = qb.shape[0]
    groups = qs.shape[2] // 128
    nsegs = nseg + len(f_refs)

    copies = [
        pltpu.make_async_copy(r, kb.at[pl.ds(s * seg, seg)], sems.at[s])
        for s, r in enumerate(kv_refs + f_refs)
    ]

    q_copies = [
        pltpu.make_async_copy(r, qs.at[i], q_sems.at[i]) for i, r in enumerate(q_refs)
    ]
    st_copies = [
        pltpu.make_async_copy(r, st.at[i], st_sems.at[i]) for i, r in enumerate(st_refs)
    ]

    q_copies[0].start()
    for c in copies[:1] + q_copies[1:] + st_copies + copies[1:]:
        c.start()
    for i in range(nq):
        q_copies[i].wait()
        for g in range(groups):
            at = (i * groups + g) * 128
            qb[at : at + 128, :] = qs[i, :, g * 128 : (g + 1) * 128]
    copies[0].wait()

    if state_in:
        sides = []
        for i in range(nq):
            st_copies[i].wait()
            sides.append(st[i, :, groups * 128 :].astype(F32))
            for g in range(groups):
                at = (i * groups + g) * 128
                mm[at : at + 128, :] = jnp.broadcast_to(sides[i][:, g : g + 1], (128, 128))
    else:
        top = jnp.max(nt_dot(qb[...], kb[:256, :HD]), axis=-1, keepdims=True) * SCALE
        mm[...] = jnp.broadcast_to(top.astype(BF16).astype(F32), mm.shape)

    def up_to(limit, size):
        col = lax.broadcasted_iota(jnp.int32, (8, size), 1)
        return (col <= limit)[:1]

    def not_after():
        col = lax.broadcasted_iota(jnp.int32, (rows, 128), 1)
        row = lax.rem(lax.broadcasted_iota(jnp.int32, (rows, 128), 0), 128)
        return col <= row

    def accumulate(at, size, seen=None):
        at = pl.ds(pl.multiple_of(at, 128), size)
        s = nt_dot(qb[...], kb[at, :HD])
        tops = jnp.concatenate([mm[...]] * (size // 128), axis=1)
        p = jnp.exp2(s * SCALE - tops)
        if seen is not None:
            p = jnp.where(seen, p, 0.0)
        acc[...] += nn_dot(p.astype(BF16), kb[at, HD:])
        total = ll[...]
        for g in range(size // 128):
            total = total + p[:, g * 128 : (g + 1) * 128]
        ll[...] = total

    def segment(s):
        owner = me ^ owner_xor[0]
        for i in range(1, nseg):
            owner = jnp.where(s == i, me ^ owner_xor[i], owner)
        length = jnp.clip(len_ref[owner], 0, seg)
        if fresh:
            length = jnp.where(s == nseg, me * 128, length)
        whole = length // 512 * 512
        return s * seg, whole, length - whole

    diagonal = nseg * seg + me * 128

    def sweep(turn):
        acc[...] = jnp.zeros_like(acc)
        ll[...] = jnp.zeros_like(ll)

        def one(s, carry):
            start, whole, rest = segment(s)

            for i in range(1, nsegs):

                @pl.when((s == i) & (turn == 0))
                def _():
                    copies[i].wait()

            wide = whole // 1024

            def wide_step(j, c):
                accumulate(start + j * 1024, 1024)
                return c

            lax.fori_loop(0, wide, wide_step, 0)

            @pl.when(whole > wide * 1024)
            def _():
                accumulate(start + wide * 1024, 512)

            @pl.when(rest > 256)
            def _():
                accumulate(start + whole, 512, up_to(rest - 1, 512))

            @pl.when((rest > 0) & (rest <= 256))
            def _():
                accumulate(start + whole, 256, up_to(rest - 1, 256))

            return carry

        lax.fori_loop(0, nsegs, one, 0)
        if fresh:
            accumulate(diagonal, 128, not_after())

    def raise_tops():
        def part(at, seen):
            at = pl.ds(pl.multiple_of(at, 128), 128)
            s_now = nt_dot(qb[...], kb[at, :HD]) * SCALE
            top = jnp.max(jnp.where(seen, s_now, -3.0e38), axis=-1, keepdims=True)
            mm[...] = jnp.maximum(mm[...], top.astype(BF16).astype(F32))

        def one(s, carry):
            start, whole, rest = segment(s)

            def step(j, c):
                part(start + j * 128, up_to(whole + rest - 1 - j * 128, 128))
                return c

            return lax.fori_loop(0, (whole + rest + 127) // 128, step, carry)

        lax.fori_loop(0, nsegs, one, 0)
        if fresh:
            part(diagonal, not_after())

    def attempt(turn):
        @pl.when(turn == 1)
        def _():
            raise_tops()

        sweep(turn)
        fits = jnp.max(ll[...]) < BIG
        return jnp.where((turn == 0) & jnp.logical_not(fits), 1, 2)

    lax.while_loop(lambda turn: turn < 2, attempt, 0)

    lane = lax.broadcasted_iota(jnp.int32, (128, 128), 1)

    for i in range(nq):
        out = outs[i]
        side = jnp.zeros((128, 128), F32)
        for g in range(groups):
            rows_at = slice((i * groups + g) * 128, (i * groups + g + 1) * 128)
            part = slice(g * 128, (g + 1) * 128)
            mixed = acc[rows_at, :]
            total = jnp.sum(ll[rows_at, :], axis=-1, keepdims=True)
            top = mm[rows_at, :]
            if state_in:
                before = sides[i]
                decay = jnp.exp2(before[:, g : g + 1] - top)
                mixed = mixed + st[i, :, part].astype(F32) * decay
                total = total + (before[:, 8 + g : 9 + g] + before[:, 16 + g : 17 + g]) * decay
            out[:, part] = mixed.astype(BF16)
            high = total.astype(BF16).astype(F32)
            side = jnp.where(lane == g, top, side)
            side = jnp.where(lane == 8 + g, high, side)
            side = jnp.where(lane == 16 + g, total - high, side)
        out[:, groups * 128 :] = side.astype(BF16)

    if fresh:
        owner_ref, slot_ref = page_refs
        (pages,) = pages_out
        pages[...] = jnp.zeros_like(pages)

        def one_page(page, carry):
            @pl.when(owner_ref[page] == me)
            def _():
                src = pl.ds(pl.multiple_of(nseg * seg + page * PAGE, PAGE), PAGE)
                dst = pl.ds(pl.multiple_of(slot_ref[page] * PAGE, PAGE), PAGE)
                pages[dst, :] = kb[src, :]

            return carry

        lax.fori_loop(0, owner_ref.shape[0], one_page, 0)


def attend(
    lengths, qs, kvs, owner_xor, state=None, fresh=None, pages=None, flops=2 * 10**10
):
    nq, nseg, seg = len(qs), len(kvs), kvs[0].shape[0]
    width = qs[0].shape[1]
    rows = nq * width
    cfg = (nq, nseg, seg, owner_xor, state is not None, fresh is not None)
    any_spec = pl.BlockSpec(memory_space=pl.ANY)
    args = [lengths, *qs, *kvs]
    in_specs = [smem_spec()] + [any_spec] * (nq + nseg)
    out_specs = [pl.BlockSpec((128, width + 128), lambda i: (0, 0))] * nq
    out_shape = [jax.ShapeDtypeStruct((128, width + 128), BF16)] * nq
    if fresh is not None:
        args += [fresh, *pages]
        in_specs += [any_spec, smem_spec(), smem_spec()]
        out_specs.append(pl.BlockSpec((8 * PAGE, 2 * HD), lambda i: (0, 0)))
        out_shape.append(jax.ShapeDtypeStruct((8 * PAGE, 2 * HD), BF16))
    if state is not None:
        args += state
        in_specs += [any_spec] * nq
    nsegs = nseg + (fresh is not None)
    return pl.pallas_call(
        functools.partial(attend_kernel, cfg),
        grid=(1,),
        in_specs=in_specs,
        out_specs=out_specs,
        out_shape=out_shape,
        scratch_shapes=[
            pltpu.VMEM((nq, 128, width), BF16),
            pltpu.VMEM((rows, HD), BF16),
            pltpu.VMEM((nsegs * seg, 2 * HD), BF16),
            pltpu.VMEM((rows, HD), F32),
            pltpu.VMEM((rows, HD), F32),
            pltpu.VMEM((rows, HD), F32),
            pltpu.VMEM((nq, 128, width + 128), BF16),
            pltpu.SemaphoreType.DMA((nsegs,)),
            pltpu.SemaphoreType.DMA((nq,)),
            pltpu.SemaphoreType.DMA((nq,)),
        ],
        compiler_params=pltpu.CompilerParams(vmem_limit_bytes=VMEM_LIMIT),
        cost_estimate=pl.CostEstimate(
            flops=flops, bytes_accessed=1000, transcendentals=0
        ),
        name="attend",
    )(*args)


def merge_kernel(*refs):
    parts, out = refs[:-1], refs[-1]
    groups = out.shape[1] // 128
    sides = [r[:, groups * 128 :].astype(F32) for r in parts]
    top = functools.reduce(jnp.maximum, sides)
    scales = [jnp.exp2(s - top) for s in sides]
    total = jnp.zeros_like(top)
    for w, s in zip(scales, sides):
        total = total + w * (pltpu.roll(s, 120, 1) + pltpu.roll(s, 112, 1))
    scales = [w / total for w in scales]
    for g in range(groups):
        part = slice(g * 128, (g + 1) * 128)
        mixed = sum(w[:, g : g + 1] * r[:, part].astype(F32) for w, r in zip(scales, parts))
        out[:, part] = mixed.astype(BF16)


def merge(parts):
    rows, width = parts[0].shape
    return pl.pallas_call(
        merge_kernel,
        grid=(2,),
        in_specs=[pl.BlockSpec((rows // 2, width), lambda i: (i, 0))] * len(parts),
        out_specs=pl.BlockSpec((rows // 2, width - 128), lambda i: (i, 0)),
        out_shape=jax.ShapeDtypeStruct((rows, width - 128), BF16),
        compiler_params=pltpu.CompilerParams(vmem_limit_bytes=VMEM_LIMIT),
        cost_estimate=SMALL,
        name="merge",
    )(*parts)


def relay_kernel(parts, spread, total, sems):
    added = parts[0].astype(F32)
    for i in range(1, parts.shape[0]):
        added = added + parts[i].astype(F32)
    total[...] = added.astype(BF16)
    copies = [
        pltpu.make_async_copy(total, spread.at[i], sems.at[i]) for i in range(spread.shape[0])
    ]
    for c in copies:
        c.start()
    for c in copies:
        c.wait()


def relay(parts, count):
    block = parts.shape[1:]
    return pl.pallas_call(
        relay_kernel,
        in_specs=[vmem_spec()],
        out_specs=pl.BlockSpec(memory_space=pl.ANY),
        out_shape=jax.ShapeDtypeStruct((count, *block), BF16),
        scratch_shapes=[pltpu.VMEM(block, BF16), pltpu.SemaphoreType.DMA((count,))],
        compiler_params=pltpu.CompilerParams(vmem_limit_bytes=VMEM_LIMIT),
        cost_estimate=pl.CostEstimate(
            flops=2 * 10**10, bytes_accessed=1000, transcendentals=0
        ),
        name="relay",
    )(parts)


def pack_kernel(k_ref, v_ref, out_ref):
    out_ref[:, :HD] = k_ref[...]
    out_ref[:, HD:] = v_ref[...]


def pack(keys, values):
    rows = keys.shape[0]
    block = pl.BlockSpec((rows // 2, HD), lambda i: (i, 0))
    return pl.pallas_call(
        pack_kernel,
        grid=(2,),
        in_specs=[block] * 2,
        out_specs=pl.BlockSpec((rows // 2, 2 * HD), lambda i: (i, 0)),
        out_shape=jax.ShapeDtypeStruct((rows, 2 * HD), BF16),
        compiler_params=pltpu.CompilerParams(vmem_limit_bytes=VMEM_LIMIT),
        cost_estimate=SMALL,
        name="pack",
    )(keys, values)


def flip(x, bits):
    return lax.ppermute(x, "ctx", [(i, i ^ bits) for i in range(16)])


def turn(x, k):
    return lax.ppermute(x, "ctx", [(i, (i + 4 * k) % 16) for i in range(16)])


def body(
    tokens, kv_weight, queries, cache_keys, cache_values, cache_lengths, page_owner, page_slot
):
    order = (1, 3, 2)
    others = [turn(queries, k) for k in order]
    own_kv = pack(cache_keys, cache_values)
    far_kv = flip(own_kv, 2)
    core_kv = flip(own_kv, 1)

    partial = project(tokens, kv_weight)
    gathered = lax.all_to_all(partial, "tp", 0, 0, tiled=True)

    near, far = (0, 1), (2, 3)
    lengths, _ = lax.optimization_barrier((cache_lengths, partial))
    nears = attend(lengths, others, (own_kv, core_kv), near, flops=FIRST)
    lengths, gathered, far_kv, _ = lax.optimization_barrier((lengths, gathered, far_kv, nears[0]))
    both_kv = flip(far_kv, 1)
    spread = relay(gathered, 16)
    fresh = lax.all_to_all(spread, "ctx", 0, 0, tiled=True).reshape(16 * 128, 2 * HD)
    sent = attend(lengths, others, (far_kv, both_kv), far, state=list(nears))
    back = [turn(part, 4 - k) for part, k in zip(sent, order)]
    lengths, _ = lax.optimization_barrier((lengths, sent[0]))
    mine, kv_pages = attend(
        lengths, [queries], (own_kv, core_kv, far_kv, both_kv), near + far, fresh=fresh,
        pages=(page_owner, page_slot),
    )
    attended = merge([mine, *back])
    return (attended, kv_pages)


def solution(mesh):
    placed = (
        P("ctx", "tp"),
        P("tp", None),
        P("ctx", "tp"),
        P("ctx", "tp"),
        P("ctx", "tp"),
        P(),
        P(),
        P(),
    )
    return jax.shard_map(
        body,
        mesh=mesh,
        in_specs=placed,
        out_specs=(P("ctx", "tp"), P("ctx", "tp")),
        check_vma=False,
    )
```

```python
import functools

import jax
import jax.numpy as jnp
from jax import lax
from jax.experimental import pallas as pl
from jax.experimental.pallas import tpu as pltpu
from jax.sharding import PartitionSpec as P

PAGE = 32
HD = 128
LOG2E = 1.4426950408889634
SCALE = LOG2E / HD**0.5
BIG = 2.0**100
F32 = jnp.float32
BF16 = jnp.bfloat16
FIRST = 4 * 10**9
VMEM_LIMIT = 63 * 2**20 + 2**19 + 2**18 + 2**17
SMALL = pl.CostEstimate(flops=1000, bytes_accessed=1000, transcendentals=0)


def nt_dot(a, b):
    return lax.dot_general(a, b, (((1,), (1,)), ((), ())), preferred_element_type=F32)


def nn_dot(a, b):
    return lax.dot_general(a, b, (((1,), (0,)), ((), ())), preferred_element_type=F32)


def vmem_spec():
    return pl.BlockSpec(memory_space=pltpu.VMEM)


def smem_spec():
    return pl.BlockSpec(memory_space=pltpu.SMEM)


def project_kernel(tok_ref, w_ref, out_ref):
    result = nn_dot(tok_ref[...], w_ref[...]).astype(BF16)
    for h in range(out_ref.shape[0]):
        out_ref[h] = result[:, h * 2 * HD : (h + 1) * 2 * HD]


def project(tokens, kv_weight):
    rows, depth = tokens.shape
    heads = kv_weight.shape[1] // (2 * HD)
    at_once = 4
    return pl.pallas_call(
        project_kernel,
        grid=(heads // at_once,),
        in_specs=[
            pl.BlockSpec((rows, depth), lambda h: (0, 0)),
            pl.BlockSpec((depth, at_once * 2 * HD), lambda h: (0, h)),
        ],
        out_specs=pl.BlockSpec((at_once, rows, 2 * HD), lambda h: (h, 0, 0)),
        out_shape=jax.ShapeDtypeStruct((heads, rows, 2 * HD), BF16),
        compiler_params=pltpu.CompilerParams(vmem_limit_bytes=VMEM_LIMIT),
        cost_estimate=SMALL,
        name="project",
    )(tokens, kv_weight)


def attend_kernel(cfg, *refs):
    nq, nseg, seg, owner_xor, state_in, fresh = cfg
    refs = list(refs)
    take = lambda n: [refs.pop(0) for _ in range(n)]
    (len_ref,) = take(1)
    q_refs = take(nq)
    kv_refs = take(nseg)
    f_refs = take(1) if fresh else []
    page_refs = take(2) if fresh else []
    st_refs = take(nq) if state_in else []
    outs = take(nq)
    pages_out = take(1) if fresh else []
    qs, qb, kb, acc, ll, mm, st, sems, q_sems, st_sems = refs
    me = lax.axis_index("ctx")
    rows = qb.shape[0]
    groups = qs.shape[2] // 128
    nsegs = nseg + len(f_refs)

    copies = [
        pltpu.make_async_copy(r, kb.at[pl.ds(s * seg, seg)], sems.at[s])
        for s, r in enumerate(kv_refs + f_refs)
    ]

    q_copies = [
        pltpu.make_async_copy(r, qs.at[i], q_sems.at[i]) for i, r in enumerate(q_refs)
    ]
    st_copies = [
        pltpu.make_async_copy(r, st.at[i], st_sems.at[i]) for i, r in enumerate(st_refs)
    ]

    q_copies[0].start()
    for c in copies[:1] + q_copies[1:] + st_copies + copies[1:]:
        c.start()
    for i in range(nq):
        q_copies[i].wait()
        for g in range(groups):
            at = (i * groups + g) * 128
            qb[at : at + 128, :] = qs[i, :, g * 128 : (g + 1) * 128]
    copies[0].wait()

    if state_in:
        sides = []
        for i in range(nq):
            st_copies[i].wait()
            sides.append(st[i, :, groups * 128 :].astype(F32))
            for g in range(groups):
                at = (i * groups + g) * 128
                mm[at : at + 128, :] = jnp.broadcast_to(sides[i][:, g : g + 1], (128, 128))
    else:
        top = jnp.max(nt_dot(qb[...], kb[:128, :HD]), axis=-1, keepdims=True) * SCALE
        mm[...] = jnp.broadcast_to(top.astype(BF16).astype(F32), mm.shape)

    def up_to(limit, size):
        col = lax.broadcasted_iota(jnp.int32, (8, size), 1)
        return (col <= limit)[:1]

    def not_after():
        col = lax.broadcasted_iota(jnp.int32, (rows, 128), 1)
        row = lax.rem(lax.broadcasted_iota(jnp.int32, (rows, 128), 0), 128)
        return col <= row

    def accumulate(at, size, seen=None):
        at = pl.ds(pl.multiple_of(at, 128), size)
        s = nt_dot(qb[...], kb[at, :HD])
        tops = jnp.concatenate([mm[...]] * (size // 128), axis=1)
        p = jnp.exp2(s * SCALE - tops)
        if seen is not None:
            p = jnp.where(seen, p, 0.0)
        acc[...] += nn_dot(p.astype(BF16), kb[at, HD:])
        total = ll[...]
        for g in range(size // 128):
            total = total + p[:, g * 128 : (g + 1) * 128]
        ll[...] = total

    def segment(s):
        owner = me ^ owner_xor[0]
        for i in range(1, nseg):
            owner = jnp.where(s == i, me ^ owner_xor[i], owner)
        length = jnp.clip(len_ref[owner], 0, seg)
        if fresh:
            length = jnp.where(s == nseg, me * 128, length)
        whole = length // 512 * 512
        return s * seg, whole, length - whole

    diagonal = nseg * seg + me * 128

    def sweep(turn):
        acc[...] = jnp.zeros_like(acc)
        ll[...] = jnp.zeros_like(ll)

        def one(s, carry):
            start, whole, rest = segment(s)

            for i in range(1, nsegs):

                @pl.when((s == i) & (turn == 0))
                def _():
                    copies[i].wait()

            wide = whole // 1024

            def wide_step(j, c):
                accumulate(start + j * 1024, 1024)
                return c

            lax.fori_loop(0, wide, wide_step, 0)

            @pl.when(whole > wide * 1024)
            def _():
                accumulate(start + wide * 1024, 512)

            @pl.when(rest > 256)
            def _():
                accumulate(start + whole, 512, up_to(rest - 1, 512))

            @pl.when((rest > 0) & (rest <= 256))
            def _():
                accumulate(start + whole, 256, up_to(rest - 1, 256))

            return carry

        lax.fori_loop(0, nsegs, one, 0)
        if fresh:
            accumulate(diagonal, 128, not_after())

    def raise_tops():
        def part(at, seen):
            at = pl.ds(pl.multiple_of(at, 128), 128)
            s_now = nt_dot(qb[...], kb[at, :HD]) * SCALE
            top = jnp.max(jnp.where(seen, s_now, -3.0e38), axis=-1, keepdims=True)
            mm[...] = jnp.maximum(mm[...], top.astype(BF16).astype(F32))

        def one(s, carry):
            start, whole, rest = segment(s)

            def step(j, c):
                part(start + j * 128, up_to(whole + rest - 1 - j * 128, 128))
                return c

            return lax.fori_loop(0, (whole + rest + 127) // 128, step, carry)

        lax.fori_loop(0, nsegs, one, 0)
        if fresh:
            part(diagonal, not_after())

    def attempt(turn):
        @pl.when(turn == 1)
        def _():
            raise_tops()
            if state_in:
                for i in range(nq):
                    for g in range(groups):
                        at = (i * groups + g) * 128
                        part = slice(g * 128, (g + 1) * 128)
                        decay = jnp.exp2(sides[i][:, g : g + 1] - mm[at : at + 128, :])
                        st[i, :, part] = (st[i, :, part].astype(F32) * decay).astype(BF16)

        sweep(turn)
        fits = jnp.max(ll[...]) < BIG
        return jnp.where((turn == 0) & jnp.logical_not(fits), 1, 2)

    lax.while_loop(lambda turn: turn < 2, attempt, 0)

    lane = lax.broadcasted_iota(jnp.int32, (128, 128), 1)

    for i in range(nq):
        out = outs[i]
        tops = jnp.zeros((128, 128), F32)
        sums = jnp.zeros((128, 128), F32)
        for g in range(groups):
            rows_at = slice((i * groups + g) * 128, (i * groups + g + 1) * 128)
            part = slice(g * 128, (g + 1) * 128)
            mixed = acc[rows_at, :]
            if state_in:
                mixed = mixed + st[i, :, part].astype(F32)
            out[:, part] = mixed.astype(BF16)
            tops = jnp.where(lane == g, mm[rows_at, :], tops)
            total = jnp.sum(ll[rows_at, :], axis=-1, keepdims=True)
            sums = jnp.where(lane == 8 + g, total, sums)
        if state_in:
            before = sides[i] + pltpu.roll(sides[i], 120, 1)
            decay = pltpu.roll(jnp.exp2(sides[i] - tops), 8, 1)
            sums = jnp.where((lane >= 8) & (lane < 16), sums + before * decay, 0.0)
        high = sums.astype(BF16).astype(F32)
        side = tops + high + pltpu.roll(sums - high, 8, 1)
        out[:, groups * 128 :] = side.astype(BF16)

    if fresh:
        owner_ref, slot_ref = page_refs
        (pages,) = pages_out
        pages[...] = jnp.zeros_like(pages)

        def one_page(page, carry):
            @pl.when(owner_ref[page] == me)
            def _():
                src = pl.ds(pl.multiple_of(nseg * seg + page * PAGE, PAGE), PAGE)
                dst = pl.ds(pl.multiple_of(slot_ref[page] * PAGE, PAGE), PAGE)
                pages[dst, :] = kb[src, :]

            return carry

        lax.fori_loop(0, owner_ref.shape[0], one_page, 0)


def attend(
    lengths, qs, kvs, owner_xor, state=None, fresh=None, pages=None, flops=2 * 10**10
):
    nq, nseg, seg = len(qs), len(kvs), kvs[0].shape[0]
    width = qs[0].shape[1]
    rows = nq * width
    cfg = (nq, nseg, seg, owner_xor, state is not None, fresh is not None)
    any_spec = pl.BlockSpec(memory_space=pl.ANY)
    args = [lengths, *qs, *kvs]
    in_specs = [smem_spec()] + [any_spec] * (nq + nseg)
    out_specs = [pl.BlockSpec((128, width + 128), lambda i: (0, 0))] * nq
    out_shape = [jax.ShapeDtypeStruct((128, width + 128), BF16)] * nq
    if fresh is not None:
        args += [fresh, *pages]
        in_specs += [any_spec, smem_spec(), smem_spec()]
        out_specs.append(pl.BlockSpec((8 * PAGE, 2 * HD), lambda i: (0, 0)))
        out_shape.append(jax.ShapeDtypeStruct((8 * PAGE, 2 * HD), BF16))
    if state is not None:
        args += state
        in_specs += [any_spec] * nq
    nsegs = nseg + (fresh is not None)
    return pl.pallas_call(
        functools.partial(attend_kernel, cfg),
        grid=(1,),
        in_specs=in_specs,
        out_specs=out_specs,
        out_shape=out_shape,
        scratch_shapes=[
            pltpu.VMEM((nq, 128, width), BF16),
            pltpu.VMEM((rows, HD), BF16),
            pltpu.VMEM((nsegs * seg, 2 * HD), BF16),
            pltpu.VMEM((rows, HD), F32),
            pltpu.VMEM((rows, HD), F32),
            pltpu.VMEM((rows, HD), F32),
            pltpu.VMEM((nq, 128, width + 128), BF16),
            pltpu.SemaphoreType.DMA((nsegs,)),
            pltpu.SemaphoreType.DMA((nq,)),
            pltpu.SemaphoreType.DMA((nq,)),
        ],
        compiler_params=pltpu.CompilerParams(vmem_limit_bytes=VMEM_LIMIT),
        cost_estimate=pl.CostEstimate(
            flops=flops, bytes_accessed=1000, transcendentals=0
        ),
        name="attend",
    )(*args)


def merge_kernel(*refs):
    parts, out = refs[:-1], refs[-1]
    groups = out.shape[1] // 128
    sides = [r[:, groups * 128 :].astype(F32) for r in parts]
    top = functools.reduce(jnp.maximum, sides)
    scales = [jnp.exp2(s - top) for s in sides]
    total = jnp.zeros_like(top)
    for w, s in zip(scales, sides):
        total = total + w * (pltpu.roll(s, 120, 1) + pltpu.roll(s, 112, 1))
    scales = [w / total for w in scales]
    for g in range(groups):
        part = slice(g * 128, (g + 1) * 128)
        mixed = sum(w[:, g : g + 1] * r[:, part].astype(F32) for w, r in zip(scales, parts))
        out[:, part] = mixed.astype(BF16)


def merge(parts):
    rows, width = parts[0].shape
    return pl.pallas_call(
        merge_kernel,
        grid=(2,),
        in_specs=[pl.BlockSpec((rows // 2, width), lambda i: (i, 0))] * len(parts),
        out_specs=pl.BlockSpec((rows // 2, width - 128), lambda i: (i, 0)),
        out_shape=jax.ShapeDtypeStruct((rows, width - 128), BF16),
        compiler_params=pltpu.CompilerParams(vmem_limit_bytes=VMEM_LIMIT),
        cost_estimate=SMALL,
        name="merge",
    )(*parts)


def relay_kernel(parts, spread, total, sems):
    added = parts[0].astype(F32)
    for i in range(1, parts.shape[0]):
        added = added + parts[i].astype(F32)
    total[...] = added.astype(BF16)
    copies = [
        pltpu.make_async_copy(total, spread.at[i], sems.at[i]) for i in range(spread.shape[0])
    ]
    for c in copies:
        c.start()
    for c in copies:
        c.wait()


def relay(parts, count):
    block = parts.shape[1:]
    return pl.pallas_call(
        relay_kernel,
        in_specs=[vmem_spec()],
        out_specs=pl.BlockSpec(memory_space=pl.ANY),
        out_shape=jax.ShapeDtypeStruct((count, *block), BF16),
        scratch_shapes=[pltpu.VMEM(block, BF16), pltpu.SemaphoreType.DMA((count,))],
        compiler_params=pltpu.CompilerParams(vmem_limit_bytes=VMEM_LIMIT),
        cost_estimate=pl.CostEstimate(
            flops=2 * 10**10, bytes_accessed=1000, transcendentals=0
        ),
        name="relay",
    )(parts)


def pack_kernel(k_ref, v_ref, out_ref):
    out_ref[:, :HD] = k_ref[...]
    out_ref[:, HD:] = v_ref[...]


def pack(keys, values):
    rows = keys.shape[0]
    block = pl.BlockSpec((rows // 2, HD), lambda i: (i, 0))
    return pl.pallas_call(
        pack_kernel,
        grid=(2,),
        in_specs=[block] * 2,
        out_specs=pl.BlockSpec((rows // 2, 2 * HD), lambda i: (i, 0)),
        out_shape=jax.ShapeDtypeStruct((rows, 2 * HD), BF16),
        compiler_params=pltpu.CompilerParams(vmem_limit_bytes=VMEM_LIMIT),
        cost_estimate=SMALL,
        name="pack",
    )(keys, values)


def flip(x, bits):
    return lax.ppermute(x, "ctx", [(i, i ^ bits) for i in range(16)])


def turn(x, k):
    return lax.ppermute(x, "ctx", [(i, (i + 4 * k) % 16) for i in range(16)])


def body(
    tokens, kv_weight, queries, cache_keys, cache_values, cache_lengths, page_owner, page_slot
):
    order = (1, 3, 2)
    others = [turn(queries, k) for k in order]
    own_kv = pack(cache_keys, cache_values)
    far_kv = flip(own_kv, 2)
    core_kv = flip(own_kv, 1)

    partial = project(tokens, kv_weight)
    gathered = lax.all_to_all(partial, "tp", 0, 0, tiled=True)

    near, far = (0, 1), (2, 3)
    lengths, _ = lax.optimization_barrier((cache_lengths, partial))
    nears = attend(lengths, others, (own_kv, core_kv), near, flops=FIRST)
    lengths, gathered, far_kv, _ = lax.optimization_barrier((lengths, gathered, far_kv, nears[0]))
    both_kv = flip(far_kv, 1)
    spread = relay(gathered, 16)
    fresh = lax.all_to_all(spread, "ctx", 0, 0, tiled=True).reshape(16 * 128, 2 * HD)
    sent = attend(lengths, others, (far_kv, both_kv), far, state=list(nears))
    back = [turn(part, 4 - k) for part, k in zip(sent, order)]
    lengths, _ = lax.optimization_barrier((lengths, sent[0]))
    mine, kv_pages = attend(
        lengths, [queries], (own_kv, core_kv, far_kv, both_kv), near + far, fresh=fresh,
        pages=(page_owner, page_slot),
    )
    attended = merge([mine, *back])
    return (attended, kv_pages)


def solution(mesh):
    placed = (
        P("ctx", "tp"),
        P("tp", None),
        P("ctx", "tp"),
        P("ctx", "tp"),
        P("ctx", "tp"),
        P(),
        P(),
        P(),
    )
    return jax.shard_map(
        body,
        mesh=mesh,
        in_specs=placed,
        out_specs=(P("ctx", "tp"), P("ctx", "tp")),
        check_vma=False,
    )
```
